128 devices in a mesh: wide: 32 (over x, z, core), narrow: 4 (over y).
Axes of the slice: x: 4, y: 4, z: 4, core: 2. Of those that a mesh axis runs over, the one named last changes fastest.
Arguments:
- points: bfloat16 [131072, 256], P('wide'), may hold values from -6 to 6
- q_init: float32 [16, 131072], P(None, 'wide'), may hold values from -80 to 80
- pairs: int32 [2, 8192], P(None, ('wide', 'narrow')), may hold values from 0 to 1023, as said below
Outputs:
- basis: float32 [16, 131072], P(None, 'wide')
- coeffs: float32 [3, 2, 16, 16], replicated
The draws below stay inside these ranges and needn't reach their ends.
Inputs may be any that keep to these rules, and one draw needn't show every extreme that they name: `pairs`: pair number g * 4 * 64 + m * 64 + o * 2 + c (g < 32, m < 4, o < 32, c < 2) has its first block in g * 32 .. (g + 1) * 32 - 1 and its second block in o * 32 .. (o + 1) * 32 - 1; the two ends of a pair differ.
All inputs are finite; a program needn't handle non-finite values.
Results may differ from the reference program's by a relative error of at most 0.0015.
Values may be sent and summed in bfloat16 or wider, within the bound.
No kernel may reach another device: no remote copies, remote signals or barrier semaphores. Data moves between devices by JAX's collectives and lax.ppermute only.
A program may use at most 64 MiB of HBM per device.

```python
import jax
import jax.numpy as jnp
from jax import lax

F = 256
R = 16
BS = 128
STEPS = 3
PAIRS_DEV = 64
BLOCKS_PER_SHARD = 32
CAP = 2
NB = 1024
NPTS = 131072
TOTAL_PAIRS = 8192
N_NARROW = 4


def draw_pairs(key, part):
    slot = jnp.arange(TOTAL_PAIRS, dtype=jnp.int32)
    device = slot // PAIRS_DEV
    group = device // N_NARROW
    owner = slot % PAIRS_DEV // CAP
    first_row = jax.random.randint(jax.random.fold_in(key, 11), (TOTAL_PAIRS,), 0, BLOCKS_PER_SHARD, dtype=jnp.int32)
    offset = jax.random.randint(jax.random.fold_in(key, 12), (TOTAL_PAIRS,), 1, BLOCKS_PER_SHARD, dtype=jnp.int32)
    other = jax.random.randint(jax.random.fold_in(key, 13), (TOTAL_PAIRS,), 0, BLOCKS_PER_SHARD, dtype=jnp.int32)
    second_row = jnp.where(owner == group, (first_row + offset) % BLOCKS_PER_SHARD, other)
    first_id = group * BLOCKS_PER_SHARD + first_row
    second_id = owner * BLOCKS_PER_SHARD + second_row
    return jnp.stack([first_id, second_id]).astype(jnp.int32)


def draw_q_init(key, part):
    noise = jax.random.normal(jax.random.fold_in(key, 21), (R, NPTS), jnp.float32)
    noise = jnp.clip(noise, -6.0, 6.0)
    scales = jnp.exp(jax.random.uniform(jax.random.fold_in(key, 22), (1, NPTS), jnp.float32, 0.0, 2.3))
    values = scales * noise
    return jnp.clip(values, -80.0, 80.0).astype(jnp.float32)


def level_of(stream_key, extent, cuts, low, largest):
    loudness = 1.0
    for position, shards_of in cuts:
        steps = jax.random.uniform(jax.random.fold_in(jax.random.fold_in(stream_key, 6), position), (shards_of,), jnp.float32, low / len(cuts), largest / len(cuts))
        loudness = loudness * jnp.repeat(jnp.exp(steps), extent[position] // shards_of).reshape((-1,) + (1,) * (len(extent) - 1 - position))
    return loudness


def centred(rng, extent, deviation, limit, cuts=(), kind=jnp.bfloat16):
    entries = deviation * jax.random.normal(rng, extent, jnp.float32)
    if cuts:
        entries = entries * level_of(rng, extent, cuts, -0.22, 0.18)
    return jnp.clip(entries, -limit, limit).astype(kind)


def setup_inputs(seed: int = 0) -> dict:
    keys = jax.random.split(jax.random.key(seed), 4)
    points = centred(keys[0], (NPTS, F), 1.0, 6.0, ((0, 32),))
    q_init = draw_q_init(jax.random.fold_in(keys[3], 71), 0)
    pairs = draw_pairs(jax.random.fold_in(keys[3], 71), 0)
    return {"points": points, "q_init": q_init, "pairs": pairs}


KERNEL_FACTOR = 3.0
EPSILON = 1e-06
HIGH = lax.Precision.HIGHEST

def unit_rows(points):
    wide32 = points.astype(jnp.float32)
    scaled = wide32 * lax.rsqrt(lax.optimization_barrier(jnp.sum(wide32 * wide32, axis=-1, keepdims=True)) + EPSILON)
    return scaled.astype(jnp.bfloat16)

def apply_kernel(unit, vectors, pairs):
    rows = vectors.reshape(R, NB, BS).transpose(1, 0, 2)
    point_groups = pairs.reshape(2, TOTAL_PAIRS // PAIRS_DEV, PAIRS_DEV).transpose(1, 0, 2)

    def single_group(total, ends):
        first = ends[0]
        second = ends[1]
        inner_products = jnp.einsum('paf,pbf->pab', unit[first].astype(jnp.float32), unit[second].astype(jnp.float32), precision=HIGH)
        kernel_values = jnp.exp(KERNEL_FACTOR * (inner_products - 1.0))
        to_first = jnp.einsum('pab,prb->pra', kernel_values, rows[second], precision=HIGH)
        to_second = jnp.einsum('pab,pra->prb', kernel_values, rows[first], precision=HIGH)
        return (total.at[first].add(to_first).at[second].add(to_second), None)
    total = lax.scan(single_group, jnp.zeros_like(rows), point_groups)[0]
    return total.transpose(1, 0, 2).reshape(R, NPTS)

def reference(points, q_init, pairs):
    unit = unit_rows(points).reshape(NB, BS, F)
    gram0 = jnp.dot(q_init, q_init.T, precision=HIGH) / NPTS
    factor0 = jnp.linalg.cholesky(gram0)
    current = lax.linalg.triangular_solve(factor0, q_init, left_side=True, lower=True)
    previous = jnp.zeros_like(current)
    last = jnp.zeros((R, R), jnp.float32).astype(current.dtype)
    records = []
    for step in range(STEPS):
        image = apply_kernel(unit, current, pairs)
        residual = image - jnp.dot(last.T, previous, precision=HIGH)
        along = jnp.dot(current, residual.T, precision=HIGH) / NPTS
        remainder = residual - jnp.dot(along.T, current, precision=HIGH)
        gram = jnp.dot(remainder, remainder.T, precision=HIGH) / NPTS
        factor = jnp.linalg.cholesky(gram)
        records.append(jnp.stack([along, factor]))
        previous = current
        last = factor
        current = lax.linalg.triangular_solve(factor, remainder, left_side=True, lower=True)
    return (current, jnp.stack(records))
```

```python
import functools

import jax
import jax.numpy as jnp
from jax import lax
from jax.experimental import pallas as pl
from jax.experimental.pallas import tpu as pltpu
from jax.sharding import PartitionSpec as P

BS = 128
STEPS = 3
KERNEL_FACTOR = 3.0
EPSILON = 1e-06
HIGH = lax.Precision.HIGHEST
VMEM_LIMIT = 48 * 2**20
TAIL = 8
BF = jnp.bfloat16
F32 = jnp.float32
NT = (((1,), (1,)), ((), ()))
TN = (((0,), (0,)), ((), ()))
NN = (((1,), (0,)), ((), ()))


def mm(a, b, dims):
    return lax.dot_general(a, b, dims, precision=HIGH, preferred_element_type=F32)


def mb(a, b, dims):
    return lax.dot_general(a, b, dims, preferred_element_type=F32)


def split(x):
    high = x.astype(BF)
    return high, (x - high.astype(F32)).astype(BF)


def fold(m):
    return jnp.concatenate([m[:8], m[8:], jnp.zeros((8, 96), F32)], axis=1)


def unfold(t):
    return jnp.concatenate([t[:, :16], t[:, 16:32]], axis=0)


def block(i):
    return pl.ds(pl.multiple_of(i * BS, BS), BS)


def factor_of(gram):
    n = gram.shape[0]
    rows = lax.broadcasted_iota(jnp.int32, (n, n), 0)
    cols = lax.broadcasted_iota(jnp.int32, (n, n), 1)
    low = jnp.zeros((n, n), F32)
    inverse = (rows == cols).astype(F32)
    left = gram
    for j in range(n):
        root = jnp.sqrt(left[j : j + 1, j : j + 1])
        scale = 1.0 / root
        column = jnp.where(rows >= j, left[:, j : j + 1] * scale, 0.0)
        low = jnp.where(cols == j, column, low)
        line = inverse[j : j + 1, :] * scale
        below = jnp.where(rows > j, column, 0.0)
        left = left - below * (left[j : j + 1, :] * scale)
        inverse = jnp.where(rows == j, line, inverse - below * line)
    return low, inverse


def pair_terms(tile, first, second):
    t_high, t_low = split(tile)
    f_high, f_low = first
    s_high, s_low = second
    rows = f_high.shape[0]
    a = mb(jnp.concatenate([s_high, s_low], axis=0), t_high, NT)
    to_first = a[:rows] + a[rows:] + mb(s_high, t_low, NT)
    b = mb(jnp.concatenate([f_high, f_low], axis=0), t_high, NN)
    to_second = b[:rows] + b[rows:] + mb(f_high, t_low, NN)
    return to_first, to_second


def start_kernel(wide, cap, first_ids, second_ids, points, q, unit, out, vec, meta, sem):
    own_blocks = points.shape[0] // BS
    slot_rows = BS + q.shape[0]

    def normalise(b, carry):
        rows = block(b)
        x = points[rows, :].astype(F32)
        x = x * lax.rsqrt(jnp.sum(x * x, axis=-1, keepdims=True) + EPSILON)
        unit[rows, :] = x.astype(BF)
        high, low = split(q[:, rows])
        vec[b] = jnp.concatenate([high, low], axis=1)
        return carry

    lax.fori_loop(0, own_blocks, normalise, 0, unroll=4)

    def send(p, carry):
        ids = [jnp.full((16, BS), second_ids[p * cap + c].astype(F32)) for c in range(2)]
        meta[p] = jnp.concatenate(ids, axis=1).astype(BF)
        for c in range(cap):
            i = first_ids[p * cap + c]
            pltpu.make_async_copy(
                unit.at[block(i), :], out.at[p, pl.ds(c * slot_rows, BS), :], sem
            ).start()
            pltpu.make_async_copy(
                vec.at[i], out.at[p, pl.ds(c * slot_rows + BS, 16), :], sem
            ).start()
        pltpu.make_async_copy(meta.at[p], out.at[p, pl.ds(cap * slot_rows, 16), :], sem).start()
        return carry

    lax.fori_loop(0, wide, send, 0)
    pltpu.make_async_copy(out, out, sem).wait()


def tiles_kernel(peers, cap, ids, got, unit, q, tiles, back, total, gram):
    step = pl.program_id(0)
    vec_rows = q.shape[0]
    slot_rows = BS + vec_rows

    @pl.when(step == 0)
    def _():
        total[...] = jnp.zeros_like(total)
        gram[...] = fold(mm(q[...], q[...], NT))

    for p in range(peers):
        for c in range(cap):
            j = ids[(step * peers + p) * cap + c]
            at = c * slot_rows
            inner = mb(got[p, at : at + BS, :], unit[block(j), :], NT)
            tile = jnp.exp(KERNEL_FACTOR * (inner - 1.0))
            tiles[p * cap + c] = tile
            first = (got[p, at + BS : at + slot_rows, :BS], got[p, at + BS : at + slot_rows, BS:])
            to_first, to_second = pair_terms(tile, first, split(q[:, block(j)]))
            back[p, c * vec_rows : (c + 1) * vec_rows, :] = to_first
            total[:, block(j)] += to_second
        back[p, cap * vec_rows :, :] = gram[...]


def terms_kernel(peers, cap, points, ids, got, tiles, w0, q, back, total, w1, along, gram):
    step = pl.program_id(0)
    vec_rows = q.shape[0]

    @pl.when(step == 0)
    def _():
        total[...] = jnp.zeros_like(total)
        a = unfold(jnp.sum(got[:, cap * vec_rows :, :], axis=0)) * (1.0 / points)
        along[...] = a
        rest = w0[...] - mm(a, q[...], TN)
        w1[...] = rest
        gram[...] = fold(mm(rest, rest, NT))

    for p in range(peers):
        for c in range(cap):
            slot = step * peers + p
            j = ids[slot * cap + c]
            first = split(got[slot, pl.ds(c * vec_rows, vec_rows), :])
            to_first, to_second = pair_terms(tiles[p * cap + c], first, split(w0[:, block(j)]))
            back[p, c * vec_rows : (c + 1) * vec_rows, :] = to_first
            total[:, block(j)] += to_second
        back[p, cap * vec_rows :, :] = gram[...]


def sum_kernel(cap, ids, got, total, out, gram):
    wide = got.shape[0]
    vec_rows = total.shape[0]
    out[...] = total[...]

    def add(p, carry):
        for c in range(cap):
            out[:, block(ids[p * cap + c])] += got[p, c * vec_rows : (c + 1) * vec_rows, :]
        return carry

    lax.fori_loop(0, wide, add, 0, unroll=4)
    gram[...] = jnp.sum(got[:, cap * vec_rows :, :], axis=0)


def factor_kernel(points, gram, low, inverse):
    low[...], inverse[...] = factor_of(unfold(gram[...]) * (1.0 / points))


def pack(cap, ids, out, vectors, matrix):
    vec_rows = vectors.shape[0]
    wide = out.shape[0]

    def put(p, carry):
        for c in range(cap):
            out[p, c * vec_rows : (c + 1) * vec_rows, :] = vectors[:, block(ids[p * cap + c])]
        out[p, cap * vec_rows :, :] = matrix
        return carry

    lax.fori_loop(0, wide, put, 0, unroll=4)


def first_update_kernel(cap, ids, t0, t1, t2, t3, q_init, inverse, q, w0, out):
    image = (t0[...] + t2[...]) + (t1[...] + t3[...])
    inv = inverse[...]
    current = mm(inv, q_init[...], NN)
    image = mm(inv, image, NN)
    q[...] = current
    w0[...] = image
    pack(cap, ids, out, w0, fold(mm(current, image, NT)))


def update_kernel(cap, ids, t0, t1, t2, t3, w1, y_old, q_old, along, low, inverse, q, w0, y, out):
    image = (t0[...] + t2[...]) + (t1[...] + t3[...])
    inv = inverse[...]
    current = mm(inv, w1[...], NN)
    image = mm(inv, image - mm(along[...], y_old[...], TN), NN)
    residual = image - mm(low[...], q_old[...], TN)
    q[...] = current
    w0[...] = residual
    y[...] = image
    matrix = fold(mm(current, residual, NT))
    if cap:
        pack(cap, ids, out, w0, matrix)
    else:
        out[...] = jnp.broadcast_to(matrix[None], out.shape)


def last_along_kernel(points, got, w0, q, w1, along, out):
    a = unfold(jnp.sum(got[...], axis=0)) * (1.0 / points)
    along[...] = a
    rest = w0[...] - mm(a, q[...], TN)
    w1[...] = rest
    out[...] = jnp.broadcast_to(fold(mm(rest, rest, NT))[None], out.shape)


def finish_kernel(points, got, w1, a0, l0, a1, l1, a2, basis, coeffs):
    low, inv = factor_of(unfold(jnp.sum(got[...], axis=0)) * (1.0 / points))
    basis[...] = mm(inv, w1[...], NN)
    for k, m in enumerate((a0, l0, a1, l1, a2)):
        coeffs[k // 2, k % 2] = m[...]
    coeffs[2, 1] = low


def call(kernel, outs, n_ids=0, **more):
    params = pltpu.CompilerParams(vmem_limit_bytes=VMEM_LIMIT)
    shapes = tuple(jax.ShapeDtypeStruct(s, d) for s, d in outs)
    if "grid" in more:
        return pl.pallas_call(
            kernel,
            out_shape=shapes,
            grid_spec=pltpu.PrefetchScalarGridSpec(num_scalar_prefetch=n_ids, **more),
            compiler_params=params,
        )

    def run(*args):
        places = [pl.BlockSpec(memory_space=pltpu.SMEM)] * n_ids
        places += [pl.BlockSpec(memory_space=pltpu.VMEM)] * (len(args) - n_ids)
        given = dict(more)
        given.setdefault("out_specs", tuple(pl.BlockSpec(memory_space=pltpu.VMEM) for _ in outs))
        return pl.pallas_call(
            kernel, out_shape=shapes, in_specs=places, compiler_params=params, **given
        )(*args)

    return run


def per_device(points, q_init, pairs):
    wide = lax.axis_size("wide")
    narrow = lax.axis_size("narrow")
    own_points, width = points.shape
    own_blocks = own_points // BS
    vec_rows = q_init.shape[0]
    pair_count = pairs.shape[1]
    cap = pair_count // wide
    total_points = own_points * wide
    local = pairs % own_blocks
    first_ids, second_ids = local[0], local[1]
    slot_rows = BS + vec_rows
    start_rows = cap * slot_rows + 16
    back_rows = cap * vec_rows + TAIL
    peers = min(4, wide)
    vectors = ((vec_rows, own_points), F32)
    small = ((vec_rows, vec_rows), F32)
    payload = ((wide, back_rows, BS), F32)
    tail = ((wide, TAIL, BS), F32)

    def exchange(x):
        return lax.all_to_all(x, "wide", split_axis=0, concat_axis=0, tiled=True)

    unit, sent = call(
        functools.partial(start_kernel, wide, cap),
        [((own_points, width), BF), ((wide, start_rows, width), BF)],
        2,
        out_specs=(pl.BlockSpec(memory_space=pltpu.VMEM), pl.BlockSpec(memory_space=pl.ANY)),
        scratch_shapes=[
            pltpu.VMEM((own_blocks, vec_rows, 2 * BS), BF),
            pltpu.VMEM((wide, 16, width), BF),
            pltpu.SemaphoreType.DMA,
        ],
    )(first_ids, second_ids, points, q_init)
    got = exchange(sent)
    ids = got[:, cap * slot_rows, ::BS].astype(jnp.int32).reshape(pair_count)

    def whole(shape):
        return pl.BlockSpec(shape, lambda i, *_: (0,) * len(shape))

    def part(shape):
        return pl.BlockSpec(shape, lambda i, *_: (i,) + (0,) * (len(shape) - 1))

    tile_part = part((peers * cap, BS, BS))
    back_part = part((peers, back_rows, BS))
    gram_scratch = [pltpu.VMEM((TAIL, BS), F32)]
    tiles, back, total = call(
        functools.partial(tiles_kernel, peers, cap),
        [((pair_count, BS, BS), F32), payload, vectors],
        1,
        grid=(wide // peers,),
        in_specs=[part((peers, start_rows, width)), whole(unit.shape), whole(q_init.shape)],
        out_specs=(tile_part, back_part, whole(q_init.shape)),
        scratch_shapes=gram_scratch,
    )(ids, got, unit, q_init)

    def gathered_sums(back, total):
        total, gram = call(
            functools.partial(sum_kernel, cap), [vectors, ((TAIL, BS), F32)], 1
        )(first_ids, exchange(back), total)
        others = [
            lax.ppermute(total, "narrow", [(i, (i + s) % narrow) for i in range(narrow)])
            for s in range(1, narrow)
        ]
        low, inverse = call(functools.partial(factor_kernel, total_points), [small, small])(gram)
        return (total, *others), low, inverse

    sums, _, inverse = gathered_sums(back, total)
    q, w0, out = call(
        functools.partial(first_update_kernel, cap), [vectors, vectors, payload], 1
    )(first_ids, *sums, q_init, inverse)
    y = w0
    records = []
    for step in range(1, STEPS):
        back, total, w1, along = call(
            functools.partial(terms_kernel, peers, cap, total_points),
            [payload, vectors, vectors, small],
            1,
            grid=(wide // peers,),
            in_specs=[
                whole(payload[0]),
                tile_part,
                whole(q_init.shape),
                whole(q_init.shape),
            ],
            out_specs=(back_part, whole(q_init.shape), whole(q_init.shape), whole(small[0])),
            scratch_shapes=gram_scratch,
        )(ids, exchange(out), tiles, w0, q)
        sums, low, inverse = gathered_sums(back, total)
        last = step == STEPS - 1
        q, w0, y, out = call(
            functools.partial(update_kernel, 0 if last else cap),
            [vectors, vectors, vectors, tail if last else payload],
            1,
        )(first_ids, *sums, w1, y, q, along, low, inverse)
        records += [along, low]
    w1, along, out = call(
        functools.partial(last_along_kernel, total_points), [vectors, small, tail]
    )(exchange(out), w0, q)
    return call(
        functools.partial(finish_kernel, total_points),
        [vectors, ((STEPS, 2, vec_rows, vec_rows), F32)],
    )(exchange(out), w1, *records, along)


def solution(mesh):
    placed = (P("wide", None), P(None, "wide"), P(None, ("wide", "narrow")))
    return jax.shard_map(
        per_device, mesh=mesh, in_specs=placed, out_specs=(P(None, "wide"), P()), check_vma=False
    )
```

```python
import functools

import jax
import jax.numpy as jnp
from jax import lax
from jax.experimental import pallas as pl
from jax.experimental.pallas import tpu as pltpu
from jax.sharding import PartitionSpec as P

BS = 128
STEPS = 3
KERNEL_FACTOR = 3.0
EPSILON = 1e-06
HIGH = lax.Precision.HIGHEST
VMEM_LIMIT = 40 * 2**20
TAIL = 8
CHUNKS = 8
BF = jnp.bfloat16
F32 = jnp.float32
NT = (((1,), (1,)), ((), ()))
TN = (((0,), (0,)), ((), ()))
NN = (((1,), (0,)), ((), ()))
cat = jnp.concatenate


def mm(a, b, dims):
    return lax.dot_general(a, b, dims, precision=HIGH, preferred_element_type=F32)


def mb(a, b, dims):
    return lax.dot_general(a, b, dims, preferred_element_type=F32)


def split(x):
    high = x.astype(BF)
    return high, (x - high.astype(F32)).astype(BF)


def block(i):
    return pl.ds(pl.multiple_of(i * BS, BS), BS)


def apply_small(m, x):
    rows = m.shape[0]
    m_high, m_low = split(m)
    left = cat([cat([m_high, m_high], axis=1), cat([m_low, jnp.zeros_like(m_low)], axis=1)], axis=0)
    out = mb(left, cat(split(x), axis=0), NN)
    return out[:rows] + out[rows:]


def factor_of(gram):
    n = gram.shape[0]
    rows = lax.broadcasted_iota(jnp.int32, (n, n), 0)
    cols = lax.broadcasted_iota(jnp.int32, (n, n), 1)
    low = jnp.zeros((n, n), F32)
    inverse = (rows == cols).astype(F32)
    left = gram
    for j in range(n):
        scale = 1.0 / jnp.sqrt(left[j : j + 1, j : j + 1])
        column = jnp.where(rows >= j, left[:, j : j + 1] * scale, 0.0)
        low = jnp.where(cols == j, column, low)
        line = inverse[j : j + 1, :] * scale
        below = jnp.where(rows > j, column, 0.0)
        left = left - below * (left[j : j + 1, :] * scale)
        inverse = jnp.where(rows == j, line, inverse - below * line)
    return low, inverse


def fold(q, w):
    n = q.shape[0]
    g = cat([q, w], axis=0)
    g = mm(g, g, NT)
    parts = (g[:n, :n], g[:n, n:], g[n:, n:])
    pieces = [p[h : h + 8] for p in parts for h in (0, 8)]
    return cat(pieces + [jnp.zeros((8, BS - 6 * n), F32)], axis=1)


def step_matrices(tails, points):
    t = jnp.sum(tails, axis=0) * (1.0 / points)
    s, a, b = (cat([t[:, 32 * k : 32 * k + 16], t[:, 32 * k + 16 : 32 * k + 32]], axis=0) for k in range(3))
    g = b - mm(a, a, TN) - mm(a, a, TN) + mm(a, mm(s, a, NN), TN)
    low, inverse = factor_of(g)
    return a, low, inverse, mm(inverse, a, NT)


def tile_stack(tile):
    return cat(split(tile), axis=0)


def pair_terms(stack, first, second):
    f_high, f_low = first
    s_high, s_low = second
    rows = f_high.shape[0]
    a = mb(cat([s_high, s_low], axis=0), stack, NT)
    to_first = a[:rows, :BS] + a[rows:, :BS] + a[:rows, BS:]
    left = cat([cat([f_high, f_high], axis=1), cat([f_low, jnp.zeros_like(f_low)], axis=1)], axis=0)
    b = mb(left, stack, NN)
    return to_first, b[:rows] + b[rows:]


def start_kernel(wide, cap, own_blocks, pairs, points, q_in, unit, out, raw, q, vec, meta, sems, sem):
    vec_rows = q.shape[0]
    slot_rows = BS + vec_rows
    size = raw.shape[0] // CHUNKS
    loads = [
        pltpu.make_async_copy(
            points.at[pl.ds(k * size, size), :], raw.at[pl.ds(k * size, size), :], sems.at[k]
        )
        for k in range(CHUNKS)
    ]
    loads.append(pltpu.make_async_copy(q_in, q, sems.at[CHUNKS]))
    for load in (loads[-1], *loads[:-1]):
        load.start()
    loads[-1].wait()
    gram = mm(q[...], q[...], NT)
    pieces = []
    for _ in range(3):
        pieces.append(gram.astype(BF).astype(F32))
        gram = gram - pieces[-1]
    sums = cat(pieces + [jnp.zeros((vec_rows, BS - 3 * vec_rows), F32)], axis=1)
    lanes = lax.broadcasted_iota(jnp.int32, sums.shape, 1)
    for b in range(own_blocks):
        vec[b] = cat(split(q[:, b * BS : (b + 1) * BS]), axis=1)

    def label(p, carry):
        ids = [lax.rem(pairs[1, p * cap + c], own_blocks).astype(F32) for c in range(cap)]
        left = jnp.where(lanes < BS // 2, sums, ids[0])
        meta[p] = cat([left, jnp.full(sums.shape, ids[1])], axis=1).astype(BF)
        return carry

    lax.fori_loop(0, wide, label, 0, unroll=4)
    for k in range(CHUNKS):
        loads[k].wait()
        for b in range(own_blocks // CHUNKS):
            rows = pl.ds(k * size + b * BS, BS)
            x = raw[rows, :].astype(F32)
            x = x * lax.rsqrt(jnp.sum(x * x, axis=-1, keepdims=True) + EPSILON)
            unit[rows, :] = x.astype(BF)

    def send(p, carry):
        for c in range(cap):
            i = lax.rem(pairs[0, p * cap + c], own_blocks)
            pltpu.make_async_copy(
                unit.at[block(i), :], out.at[p, pl.ds(c * slot_rows, BS), :], sem
            ).start()
            pltpu.make_async_copy(
                vec.at[i], out.at[p, pl.ds(c * slot_rows + BS, vec_rows), :], sem
            ).start()
        pltpu.make_async_copy(
            meta.at[p], out.at[p, pl.ds(cap * slot_rows, vec_rows), :], sem
        ).start()
        return carry

    lax.fori_loop(0, wide, send, 0)
    pltpu.make_async_copy(out, out, sem).wait()


def put_terms(terms, ids, cap, rows, back, total):
    for s, (to_first, to_second) in enumerate(terms):
        back[s // cap, (s % cap) * rows : (s % cap + 1) * rows, :] = to_first
        total[:, block(ids[s])] += to_second


def tiles_kernel(peers, cap, ids, got, unit, q, tiles, back, total, gram):
    step = pl.program_id(0)
    vec_rows = q.shape[0]
    slot_rows = BS + vec_rows
    slots = range(peers * cap)

    @pl.when(step == 0)
    def _():
        total[...] = jnp.zeros_like(total)
        gram[...] = jnp.zeros_like(gram)

    for p in range(peers):
        gram[...] += got[p, cap * slot_rows : cap * slot_rows + vec_rows, :BS].astype(F32)
    held = [ids[step * peers * cap + s] for s in slots]
    stacks = []
    for s in slots:
        at = (s % cap) * slot_rows
        inner = mb(got[s // cap, at : at + BS, :], unit[block(held[s]), :], NT)
        tile = jnp.exp(KERNEL_FACTOR * (inner - 1.0))
        tiles[s] = tile
        stacks.append(tile_stack(tile))
    terms = []
    for s in slots:
        rows = slice((s % cap) * slot_rows + BS, (s % cap + 1) * slot_rows)
        first = (got[s // cap, rows, :BS], got[s // cap, rows, BS:])
        terms.append(pair_terms(stacks[s], first, split(q[:, block(held[s])])))
    put_terms(terms, held, cap, vec_rows, back, total)


def terms_kernel(peers, cap, ids, got, tiles, w0, back, total):
    step = pl.program_id(0)
    vec_rows = w0.shape[0]

    @pl.when(step == 0)
    def _():
        total[...] = jnp.zeros_like(total)

    slots = range(peers * cap)
    held = [ids[step * peers * cap + s] for s in slots]
    terms = []
    for s in slots:
        first = got[step * peers + s // cap, pl.ds((s % cap) * vec_rows, vec_rows), :]
        second = w0[:, block(held[s])]
        terms.append(pair_terms(tile_stack(tiles[s]), split(first), split(second)))
    put_terms(terms, held, cap, vec_rows, back, total)


def sum_kernel(cap, own_blocks, pairs, got, total, out):
    vec_rows = total.shape[0]
    out[...] = total[...]

    def add(p, carry):
        for c in range(cap):
            i = lax.rem(pairs[0, p * cap + c], own_blocks)
            out[:, block(i)] += got[p, c * vec_rows : (c + 1) * vec_rows, :]
        return carry

    lax.fori_loop(0, got.shape[0], add, 0, unroll=4)


def first_factor_kernel(points, gram, matrix):
    g = gram[...]
    n = g.shape[0]
    _, inverse = factor_of((g[:, :n] + g[:, n : 2 * n] + g[:, 2 * n : 3 * n]) * (1.0 / points))
    none = jnp.zeros_like(inverse)
    matrix[...] = cat([cat([inverse, none], axis=1), cat([none, inverse], axis=1)], axis=0)


def factor_kernel(points, cap, last, got, matrix, along, low_out):
    n = along.shape[0]
    a, low, inverse, turned = step_matrices(got[:, cap * n :, :], points)
    along[...] = a
    low_out[...] = low
    none = jnp.zeros_like(low)
    across = mm(-low, (lax.broadcasted_iota(jnp.int32, (n, n), 0) == lax.broadcasted_iota(jnp.int32, (n, n), 1)).astype(F32), TN)
    lines = [cat([inverse, -turned, none, none], axis=1)]
    if not last:
        lines.append(cat([none, none, inverse, -turned], axis=1))
    lines.append(cat([none, across, inverse, -turned], axis=1))
    matrix[...] = cat(lines, axis=0)


def update_kernel(cap, own_blocks, old, pairs, t0, t1, t2, t3, *refs):
    given, matrix, outs, out = refs[:old], refs[old], refs[old + 1 : -1], refs[-1]
    image = (t0[...] + t2[...]) + (t1[...] + t3[...])
    rows = [r[...] for r in given]
    rows.insert(2 if old > 1 else 1, image)
    new = apply_small(matrix[...], cat(rows, axis=0))
    n = image.shape[0]
    for k, ref in enumerate(outs):
        ref[...] = new[k * n : (k + 1) * n]
    q, w0 = outs[0], outs[-1]
    tail = fold(new[:n], new[-n:])
    if not cap:
        out[...] = jnp.broadcast_to(tail[None], out.shape)
        return

    def put(p, carry):
        for c in range(cap):
            i = lax.rem(pairs[0, p * cap + c], own_blocks)
            out[p, c * n : (c + 1) * n, :] = w0[:, block(i)]
        out[p, cap * n :, :] = tail
        return carry

    lax.fori_loop(0, out.shape[0], put, 0, unroll=4)


def finish_kernel(points, got, w0, q, a0, l0, a1, l1, basis, coeffs):
    a, low, inverse, turned = step_matrices(got[...], points)
    basis[...] = apply_small(cat([inverse, -turned], axis=1), cat([w0[...], q[...]], axis=0))
    for k, m in enumerate((a0[...], l0[...], a1[...], l1[...], a, low)):
        coeffs[k // 2, k % 2] = m


def call(kernel, outs, n_ids=0, **more):
    params = pltpu.CompilerParams(vmem_limit_bytes=VMEM_LIMIT)
    shapes = tuple(jax.ShapeDtypeStruct(s, d) for s, d in outs)
    if "grid" in more:
        return pl.pallas_call(
            kernel,
            out_shape=shapes,
            grid_spec=pltpu.PrefetchScalarGridSpec(num_scalar_prefetch=n_ids, **more),
            compiler_params=params,
        )

    def run(*args):
        given = dict(more)
        vmem = pl.BlockSpec(memory_space=pltpu.VMEM)
        places = [pl.BlockSpec(memory_space=pltpu.SMEM)] * n_ids + [vmem] * (len(args) - n_ids)
        given.setdefault("in_specs", places)
        given.setdefault("out_specs", (vmem,) * len(outs))
        return pl.pallas_call(kernel, out_shape=shapes, compiler_params=params, **given)(*args)

    return run


def per_device(points, q_init, pairs):
    wide = lax.axis_size("wide")
    narrow = lax.axis_size("narrow")
    own_points, width = points.shape
    own_blocks = own_points // BS
    vec_rows = q_init.shape[0]
    pair_count = pairs.shape[1]
    cap = pair_count // wide
    total_points = own_points * wide
    slot_rows = BS + vec_rows
    start_rows = cap * slot_rows + vec_rows
    peers = min(8, wide)
    vectors = ((vec_rows, own_points), F32)
    small = ((vec_rows, vec_rows), F32)
    payload = ((wide, cap * vec_rows + TAIL, BS), F32)
    reply = ((wide, cap * vec_rows, BS), F32)
    tail = ((wide, TAIL, BS), F32)

    def exchange(x):
        return lax.all_to_all(x, "wide", split_axis=0, concat_axis=0, tiled=True)

    anywhere = pl.BlockSpec(memory_space=pl.ANY)
    unit, sent = call(
        functools.partial(start_kernel, wide, cap, own_blocks),
        [((own_points, width), BF), ((wide, start_rows, width), BF)],
        1,
        in_specs=[pl.BlockSpec(memory_space=pltpu.SMEM), anywhere, anywhere],
        out_specs=(pl.BlockSpec(memory_space=pltpu.VMEM), anywhere),
        scratch_shapes=[
            pltpu.VMEM((own_points, width), BF),
            pltpu.VMEM((vec_rows, own_points), F32),
            pltpu.VMEM((own_blocks, vec_rows, 2 * BS), BF),
            pltpu.VMEM((wide, vec_rows, width), BF),
            pltpu.SemaphoreType.DMA((CHUNKS + 1,)),
            pltpu.SemaphoreType.DMA,
        ],
    )(pairs, points, q_init)
    got = exchange(sent)
    labels = got[:, cap * slot_rows, BS // 2 : BS // 2 * (cap + 1) : BS // 2]
    ids = labels.astype(jnp.int32).reshape(pair_count)

    def whole(shape):
        return pl.BlockSpec(shape, lambda i, *_: (0,) * len(shape))

    def part(shape):
        return pl.BlockSpec(shape, lambda i, *_: (i,) + (0,) * (len(shape) - 1))

    tile_part = part((peers * cap, BS, BS))
    back_part = part((peers, cap * vec_rows, BS))
    tiles, back, total, gram = call(
        functools.partial(tiles_kernel, peers, cap),
        [((pair_count, BS, BS), F32), reply, vectors, ((vec_rows, BS), F32)],
        1,
        grid=(wide // peers,),
        in_specs=[part((peers, start_rows, width)), whole(unit.shape), whole(q_init.shape)],
        out_specs=(tile_part, back_part, whole(q_init.shape), whole((vec_rows, BS))),
    )(ids, got, unit, q_init)

    def narrow_terms(back, total):
        (total,) = call(functools.partial(sum_kernel, cap, own_blocks), [vectors], 1)(
            pairs, exchange(back), total
        )
        return (total,) + tuple(
            lax.ppermute(total, "narrow", [(i, (i + s) % narrow) for i in range(narrow)])
            for s in range(1, narrow)
        )

    sums = narrow_terms(back, total)
    (matrix,) = call(
        functools.partial(first_factor_kernel, total_points), [((2 * vec_rows, 2 * vec_rows), F32)]
    )(gram)
    q, w0, out = call(
        functools.partial(update_kernel, cap, own_blocks, 1), [vectors, vectors, payload], 1
    )(pairs, *sums, q_init, matrix)
    y = w0
    records = []
    for step in range(1, STEPS):
        last = step == STEPS - 1
        got = exchange(out)
        back, total = call(
            functools.partial(terms_kernel, peers, cap),
            [reply, vectors],
            1,
            grid=(wide // peers,),
            in_specs=[whole(payload[0]), tile_part, whole(q_init.shape)],
            out_specs=(back_part, whole(q_init.shape)),
        )(ids, got, tiles, w0)
        sums = narrow_terms(back, total)
        count = 2 if last else 3
        matrix, along, low = call(
            functools.partial(factor_kernel, total_points, cap, last),
            [((count * vec_rows, 4 * vec_rows), F32), small, small],
        )(got)
        *new, out = call(
            functools.partial(update_kernel, 0 if last else cap, own_blocks, 3),
            [vectors] * count + [tail if last else payload],
            1,
        )(pairs, *sums, w0, q, y, matrix)
        q, y, w0 = new[0], new[1], new[-1]
        records += [along, low]
    return call(
        functools.partial(finish_kernel, total_points),
        [vectors, ((STEPS, 2, vec_rows, vec_rows), F32)],
    )(exchange(out), w0, q, *records)


def solution(mesh):
    placed = (P("wide", None), P(None, "wide"), P(None, ("wide", "narrow")))
    return jax.shard_map(
        per_device, mesh=mesh, in_specs=placed, out_specs=(P(None, "wide"), P()), check_vma=False
    )
```

```python
import functools

import jax
import jax.numpy as jnp
from jax import lax
from jax.experimental import pallas as pl
from jax.experimental.pallas import tpu as pltpu
from jax.sharding import PartitionSpec as P

BS = 128
STEPS = 3
KERNEL_FACTOR = 3.0
EPSILON = 1e-06
HIGH = lax.Precision.HIGHEST
VMEM_LIMIT = 16 * 2**20
VMEM_START = 60 * 2**20
TAIL = 8
CHUNKS = 8
BF = jnp.bfloat16
F32 = jnp.float32
NT = (((1,), (1,)), ((), ()))
TN = (((0,), (0,)), ((), ()))
NN = (((1,), (0,)), ((), ()))
cat = jnp.concatenate


def mm(a, b, dims):
    return lax.dot_general(a, b, dims, precision=HIGH, preferred_element_type=F32)


def mb(a, b, dims):
    return lax.dot_general(a, b, dims, preferred_element_type=F32)


def split(x):
    high = x.astype(BF)
    return high, (x - high.astype(F32)).astype(BF)


def block(i):
    return pl.ds(pl.multiple_of(i * BS, BS), BS)


def apply_small(m, x):
    rows = m.shape[0]
    m_high, m_low = split(m)
    left = cat([cat([m_high, m_high], axis=1), cat([m_low, jnp.zeros_like(m_low)], axis=1)], axis=0)
    out = mb(left, cat(split(x), axis=0), NN)
    return out[:rows] + out[rows:]


def factor_of(gram):
    n = gram.shape[0]
    rows = lax.broadcasted_iota(jnp.int32, (n, n), 0)
    cols = lax.broadcasted_iota(jnp.int32, (n, n), 1)
    low = jnp.zeros((n, n), F32)
    inverse = (rows == cols).astype(F32)
    left = gram
    for j in range(n):
        scale = 1.0 / jnp.sqrt(left[j : j + 1, j : j + 1])
        column = jnp.where(rows >= j, left[:, j : j + 1] * scale, 0.0)
        low = jnp.where(cols == j, column, low)
        line = inverse[j : j + 1, :] * scale
        below = jnp.where(rows > j, column, 0.0)
        left = left - below * (left[j : j + 1, :] * scale)
        inverse = jnp.where(rows == j, line, inverse - below * line)
    return low, inverse


def fold(q, w):
    n = q.shape[0]
    g = cat([q, w], axis=0)
    g = mm(g, g, NT)
    parts = (g[:n, :n], g[:n, n:], g[n:, n:])
    pieces = [p[h : h + 8] for p in parts for h in (0, 8)]
    return cat(pieces + [jnp.zeros((8, BS - 6 * n), F32)], axis=1)


def step_matrices(tails, points):
    t = jnp.sum(tails, axis=0) * (1.0 / points)
    s, a, b = (cat([t[:, 32 * k : 32 * k + 16], t[:, 32 * k + 16 : 32 * k + 32]], axis=0) for k in range(3))
    g = b - mm(a, a, TN) - mm(a, a, TN) + mm(a, mm(s, a, NN), TN)
    low, inverse = factor_of(g)
    return a, low, inverse, mm(inverse, a, NT)


def tile_stack(tile):
    return cat(split(tile), axis=0)


def pair_terms(stack, first, second):
    f_high, f_low = first
    s_high, s_low = second
    rows = f_high.shape[0]
    a = mb(cat([s_high, s_low], axis=0), stack, NT)
    to_first = a[:rows, :BS] + a[rows:, :BS] + a[:rows, BS:]
    left = cat([cat([f_high, f_high], axis=1), cat([f_low, jnp.zeros_like(f_low)], axis=1)], axis=0)
    b = mb(left, stack, NN)
    return to_first, b[:rows] + b[rows:]


def start_kernel(wide, cap, own_blocks, pairs, points, q_in, unit, out, raw, q, vec, meta, sems, sem):
    vec_rows = q.shape[0]
    slot_rows = BS + vec_rows
    size = raw.shape[0] // CHUNKS
    loads = [
        pltpu.make_async_copy(
            points.at[pl.ds(k * size, size), :], raw.at[pl.ds(k * size, size), :], sems.at[k]
        )
        for k in range(CHUNKS)
    ]
    loads.append(pltpu.make_async_copy(q_in, q, sems.at[CHUNKS]))
    for load in loads:
        load.start()

    for k in range(CHUNKS):
        loads[k].wait()
        for b in range(own_blocks // CHUNKS):
            rows = pl.ds(k * size + b * BS, BS)
            x = raw[rows, :].astype(F32)
            x = x * lax.rsqrt(jnp.sum(x * x, axis=-1, keepdims=True) + EPSILON)
            unit[rows, :] = x.astype(BF)

    def send(p, carry):
        for c in range(cap):
            i = lax.rem(pairs[0, p * cap + c], own_blocks)
            pltpu.make_async_copy(
                unit.at[block(i), :], out.at[p, pl.ds(c * slot_rows, BS), :], sem
            ).start()
        return carry

    lax.fori_loop(0, wide, send, 0, unroll=4)
    loads[-1].wait()
    high, low = split(q[...])
    for b in range(own_blocks):
        cols = slice(b * BS, (b + 1) * BS)
        vec[b] = cat([high[:, cols], low[:, cols]], axis=1)
    both = cat([high, low], axis=0)
    gram = mb(both, both, NT)
    gram = gram[:vec_rows, :vec_rows] + (gram[:vec_rows, vec_rows:] + gram[vec_rows:, :vec_rows])
    pieces = []
    for _ in range(3):
        pieces.append(gram.astype(BF).astype(F32))
        gram = gram - pieces[-1]
    sums = cat(pieces + [jnp.zeros((vec_rows, BS - 3 * vec_rows), F32)], axis=1)
    lanes = lax.broadcasted_iota(jnp.int32, sums.shape, 1)

    def label(p, carry):
        ids = [lax.rem(pairs[1, p * cap + c], own_blocks).astype(F32) for c in range(cap)]
        left = jnp.where(lanes < BS // 2, sums, ids[0])
        meta[p] = cat([left, jnp.full(sums.shape, ids[1])], axis=1).astype(BF)
        for c in range(cap):
            i = lax.rem(pairs[0, p * cap + c], own_blocks)
            pltpu.make_async_copy(
                vec.at[i], out.at[p, pl.ds(c * slot_rows + BS, vec_rows), :], sem
            ).start()
        pltpu.make_async_copy(
            meta.at[p], out.at[p, pl.ds(cap * slot_rows, vec_rows), :], sem
        ).start()
        return carry

    lax.fori_loop(0, wide, label, 0, unroll=4)
    pltpu.make_async_copy(out, out, sem).wait()


def put_terms(terms, ids, cap, rows, back, total):
    for s, (to_first, to_second) in enumerate(terms):
        back[s // cap, (s % cap) * rows : (s % cap + 1) * rows, :] = to_first
        total[:, block(ids[s])] += to_second


def tiles_kernel(peers, cap, ids, got, unit, q, tiles, back, total, gram):
    step = pl.program_id(0)
    vec_rows = q.shape[0]
    slot_rows = BS + vec_rows
    slots = range(peers * cap)

    @pl.when(step == 0)
    def _():
        total[...] = jnp.zeros_like(total)
        gram[...] = jnp.zeros_like(gram)

    for p in range(peers):
        gram[...] += got[p, cap * slot_rows : cap * slot_rows + vec_rows, :BS].astype(F32)
    held = [ids[step * peers * cap + s] for s in slots]
    stacks = []
    for s in slots:
        at = (s % cap) * slot_rows
        inner = mb(got[s // cap, at : at + BS, :], unit[block(held[s]), :], NT)
        tile = jnp.exp(KERNEL_FACTOR * (inner - 1.0))
        tiles[s] = tile
        stacks.append(tile_stack(tile))
    terms = []
    for s in slots:
        rows = slice((s % cap) * slot_rows + BS, (s % cap + 1) * slot_rows)
        first = (got[s // cap, rows, :BS], got[s // cap, rows, BS:])
        terms.append(pair_terms(stacks[s], first, split(q[:, block(held[s])])))
    put_terms(terms, held, cap, vec_rows, back, total)


def terms_kernel(peers, cap, ids, got, tiles, w0, back, total):
    step = pl.program_id(0)
    vec_rows = w0.shape[0]

    @pl.when(step == 0)
    def _():
        total[...] = jnp.zeros_like(total)

    slots = range(peers * cap)
    held = [ids[step * peers * cap + s] for s in slots]
    terms = []
    for s in slots:
        first = got[step * peers + s // cap, pl.ds((s % cap) * vec_rows, vec_rows), :]
        second = w0[:, block(held[s])]
        terms.append(pair_terms(tile_stack(tiles[s]), split(first), split(second)))
    put_terms(terms, held, cap, vec_rows, back, total)


def sum_kernel(cap, own_blocks, pairs, got, total, out):
    vec_rows = total.shape[0]
    out[...] = total[...]

    def add(p, carry):
        for c in range(cap):
            i = lax.rem(pairs[0, p * cap + c], own_blocks)
            out[:, block(i)] += got[p, c * vec_rows : (c + 1) * vec_rows, :]
        return carry

    lax.fori_loop(0, got.shape[0], add, 0, unroll=4)


def first_factor_kernel(points, gram, matrix):
    g = gram[...]
    n = g.shape[0]
    _, inverse = factor_of((g[:, :n] + g[:, n : 2 * n] + g[:, 2 * n : 3 * n]) * (1.0 / points))
    none = jnp.zeros_like(inverse)
    matrix[...] = cat([cat([inverse, none], axis=1), cat([none, inverse], axis=1)], axis=0)


def factor_kernel(points, cap, last, got, matrix, along, low_out):
    n = along.shape[0]
    a, low, inverse, turned = step_matrices(got[:, cap * n :, :], points)
    along[...] = a
    low_out[...] = low
    none = jnp.zeros_like(low)
    across = mm(-low, (lax.broadcasted_iota(jnp.int32, (n, n), 0) == lax.broadcasted_iota(jnp.int32, (n, n), 1)).astype(F32), TN)
    lines = [cat([inverse, -turned, none, none], axis=1)]
    if not last:
        lines.append(cat([none, none, inverse, -turned], axis=1))
    lines.append(cat([none, across, inverse, -turned], axis=1))
    matrix[...] = cat(lines, axis=0)


def update_kernel(cap, own_blocks, old, pairs, t0, t1, t2, t3, *refs):
    given, matrix, outs, out = refs[:old], refs[old], refs[old + 1 : -1], refs[-1]
    image = (t0[...] + t2[...]) + (t1[...] + t3[...])
    rows = [r[...] for r in given]
    rows.insert(2 if old > 1 else 1, image)
    new = apply_small(matrix[...], cat(rows, axis=0))
    n = image.shape[0]
    for k, ref in enumerate(outs):
        ref[...] = new[k * n : (k + 1) * n]
    q, w0 = outs[0], outs[-1]
    tail = fold(new[:n], new[-n:])
    if not cap:
        out[...] = jnp.broadcast_to(tail[None], out.shape)
        return

    def put(p, carry):
        for c in range(cap):
            i = lax.rem(pairs[0, p * cap + c], own_blocks)
            out[p, c * n : (c + 1) * n, :] = w0[:, block(i)]
        out[p, cap * n :, :] = tail
        return carry

    lax.fori_loop(0, out.shape[0], put, 0, unroll=4)


def finish_kernel(points, got, w0, q, a0, l0, a1, l1, basis, coeffs):
    a, low, inverse, turned = step_matrices(got[...], points)
    basis[...] = apply_small(cat([inverse, -turned], axis=1), cat([w0[...], q[...]], axis=0))
    for k, m in enumerate((a0[...], l0[...], a1[...], l1[...], a, low)):
        coeffs[k // 2, k % 2] = m


def call(kernel, outs, n_ids=0, limit=VMEM_LIMIT, **more):
    params = pltpu.CompilerParams(vmem_limit_bytes=limit)
    shapes = tuple(jax.ShapeDtypeStruct(s, d) for s, d in outs)
    if "grid" in more:
        return pl.pallas_call(
            kernel,
            out_shape=shapes,
            grid_spec=pltpu.PrefetchScalarGridSpec(num_scalar_prefetch=n_ids, **more),
            compiler_params=params,
        )

    def run(*args):
        given = dict(more)
        vmem = pl.BlockSpec(memory_space=pltpu.VMEM)
        places = [pl.BlockSpec(memory_space=pltpu.SMEM)] * n_ids + [vmem] * (len(args) - n_ids)
        given.setdefault("in_specs", places)
        given.setdefault("out_specs", (vmem,) * len(outs))
        return pl.pallas_call(kernel, out_shape=shapes, compiler_params=params, **given)(*args)

    return run


def per_device(points, q_init, pairs):
    wide = lax.axis_size("wide")
    narrow = lax.axis_size("narrow")
    own_points, width = points.shape
    own_blocks = own_points // BS
    vec_rows = q_init.shape[0]
    pair_count = pairs.shape[1]
    cap = pair_count // wide
    total_points = own_points * wide
    slot_rows = BS + vec_rows
    start_rows = cap * slot_rows + vec_rows
    peers = min(8, wide)
    vectors = ((vec_rows, own_points), F32)
    small = ((vec_rows, vec_rows), F32)
    payload = ((wide, cap * vec_rows + TAIL, BS), F32)
    reply = ((wide, cap * vec_rows, BS), F32)
    tail = ((wide, TAIL, BS), F32)

    def exchange(x):
        return lax.all_to_all(x, "wide", split_axis=0, concat_axis=0, tiled=True)

    anywhere = pl.BlockSpec(memory_space=pl.ANY)
    unit, sent = call(
        functools.partial(start_kernel, wide, cap, own_blocks),
        [((own_points, width), BF), ((wide, start_rows, width), BF)],
        1,
        VMEM_START,
        in_specs=[pl.BlockSpec(memory_space=pltpu.SMEM), anywhere, anywhere],
        out_specs=(pl.BlockSpec(memory_space=pltpu.VMEM), anywhere),
        scratch_shapes=[
            pltpu.VMEM((own_points, width), BF),
            pltpu.VMEM((vec_rows, own_points), F32),
            pltpu.VMEM((own_blocks, vec_rows, 2 * BS), BF),
            pltpu.VMEM((wide, vec_rows, width), BF),
            pltpu.SemaphoreType.DMA((CHUNKS + 1,)),
            pltpu.SemaphoreType.DMA,
        ],
    )(pairs, points, q_init)
    got = exchange(sent)
    labels = got[:, cap * slot_rows, BS // 2 : BS // 2 * (cap + 1) : BS // 2]
    ids = labels.astype(jnp.int32).reshape(pair_count)

    def whole(shape):
        return pl.BlockSpec(shape, lambda i, *_: (0,) * len(shape))

    def part(shape):
        return pl.BlockSpec(shape, lambda i, *_: (i,) + (0,) * (len(shape) - 1))

    tile_part = part((peers * cap, BS, BS))
    back_part = part((peers, cap * vec_rows, BS))
    tiles, back, total, gram = call(
        functools.partial(tiles_kernel, peers, cap),
        [((pair_count, BS, BS), F32), reply, vectors, ((vec_rows, BS), F32)],
        1,
        grid=(wide // peers,),
        in_specs=[part((peers, start_rows, width)), whole(unit.shape), whole(q_init.shape)],
        out_specs=(tile_part, back_part, whole(q_init.shape), whole((vec_rows, BS))),
    )(ids, got, unit, q_init)

    def narrow_terms(back, total):
        (total,) = call(functools.partial(sum_kernel, cap, own_blocks), [vectors], 1)(
            pairs, exchange(back), total
        )
        return (total,) + tuple(
            lax.ppermute(total, "narrow", [(i, (i + s) % narrow) for i in range(narrow)])
            for s in range(1, narrow)
        )

    sums = narrow_terms(back, total)
    (matrix,) = call(
        functools.partial(first_factor_kernel, total_points), [((2 * vec_rows, 2 * vec_rows), F32)]
    )(gram)
    q, w0, out = call(
        functools.partial(update_kernel, cap, own_blocks, 1), [vectors, vectors, payload], 1
    )(pairs, *sums, q_init, matrix)
    y = w0
    records = []
    for step in range(1, STEPS):
        last = step == STEPS - 1
        got = exchange(out)
        back, total = call(
            functools.partial(terms_kernel, peers, cap),
            [reply, vectors],
            1,
            grid=(wide // peers,),
            in_specs=[whole(payload[0]), tile_part, whole(q_init.shape)],
            out_specs=(back_part, whole(q_init.shape)),
        )(ids, got, tiles, w0)
        sums = narrow_terms(back, total)
        count = 2 if last else 3
        matrix, along, low = call(
            functools.partial(factor_kernel, total_points, cap, last),
            [((count * vec_rows, 4 * vec_rows), F32), small, small],
        )(got)
        *new, out = call(
            functools.partial(update_kernel, 0 if last else cap, own_blocks, 3),
            [vectors] * count + [tail if last else payload],
            1,
        )(pairs, *sums, w0, q, y, matrix)
        q, y, w0 = new[0], new[1], new[-1]
        records += [along, low]
    return call(
        functools.partial(finish_kernel, total_points),
        [vectors, ((STEPS, 2, vec_rows, vec_rows), F32)],
    )(exchange(out), w0, q, *records)


def solution(mesh):
    placed = (P("wide", None), P(None, "wide"), P(None, ("wide", "narrow")))
    return jax.shard_map(
        per_device, mesh=mesh, in_specs=placed, out_specs=(P(None, "wide"), P()), check_vma=False
    )
```

```python
import functools

import jax
import jax.numpy as jnp
from jax import lax
from jax.experimental import pallas as pl
from jax.experimental.pallas import tpu as pltpu
from jax.sharding import PartitionSpec as P

BS = 128
STEPS = 3
KERNEL_FACTOR = 3.0
EPSILON = 1e-06
HIGH = lax.Precision.HIGHEST
VMEM_LIMIT = 16 * 2**20
VMEM_START = 60 * 2**20
VMEM_TILES = 30 * 2**20
TAIL = 8
CHUNKS = 8
BF = jnp.bfloat16
F32 = jnp.float32
NT = (((1,), (1,)), ((), ()))
TN = (((0,), (0,)), ((), ()))
NN = (((1,), (0,)), ((), ()))
cat = jnp.concatenate


def mm(a, b, dims):
    return lax.dot_general(a, b, dims, precision=HIGH, preferred_element_type=F32)


def mb(a, b, dims):
    return lax.dot_general(a, b, dims, preferred_element_type=F32)


def split(x):
    high = x.astype(BF)
    return high, (x - high.astype(F32)).astype(BF)


def block(i):
    return pl.ds(pl.multiple_of(i * BS, BS), BS)


def apply_small(m, x):
    rows = m.shape[0]
    m_high, m_low = split(m)
    left = cat([cat([m_high, m_high], axis=1), cat([m_low, jnp.zeros_like(m_low)], axis=1)], axis=0)
    out = mb(left, cat(split(x), axis=0), NN)
    return out[:rows] + out[rows:]


def factor_of(gram):
    n = gram.shape[0]
    rows = lax.broadcasted_iota(jnp.int32, (n, n), 0)
    cols = lax.broadcasted_iota(jnp.int32, (n, n), 1)
    same = (rows == cols).astype(F32)
    low, inverse, left = same, same, gram
    across, down = jnp.ones((1, n), F32), jnp.ones((n, 1), F32)
    for j in range(n):
        pivot = left[j : j + 1, j : j + 1]
        column = jnp.where(rows > j, left[:, j : j + 1] * (1.0 / pivot), 0.0)
        left = left - column * left[j : j + 1, :]
        inverse = inverse - column * inverse[j : j + 1, :]
        low = jnp.where(cols == j, low + column, low)
        across = jnp.where(cols[:1] == j, pivot, across)
        down = jnp.where(rows[:, :1] == j, pivot, down)
    return low * jnp.sqrt(across), inverse * (1.0 / jnp.sqrt(down))


def fold(q, w):
    n = q.shape[0]
    both = cat(split(cat([q, w], axis=0)), axis=0)
    g = mb(both, both, NT)
    g = g[: 2 * n, : 2 * n] + (g[: 2 * n, 2 * n :] + g[2 * n :, : 2 * n])
    parts = (g[:n, :n], g[:n, n:], g[n:, n:])
    pieces = [p[h : h + 8] for p in parts for h in (0, 8)]
    return cat(pieces + [jnp.zeros((8, BS - 6 * n), F32)], axis=1)


def step_matrices(tails, points):
    t = jnp.sum(tails, axis=0) * (1.0 / points)
    s, a, b = (cat([t[:, 32 * k : 32 * k + 16], t[:, 32 * k + 16 : 32 * k + 32]], axis=0) for k in range(3))
    g = b - mm(a, 2.0 * a - mm(s, a, NN), TN)
    low, inverse = factor_of(g)
    return a, low, inverse, mm(inverse, a, NT)


def tile_stack(tile):
    return cat(split(tile), axis=0)


def pair_terms(stack, first, second):
    f_high, f_low = first
    s_high, s_low = second
    rows = f_high.shape[0]
    a = mb(cat([s_high, s_low], axis=0), stack, NT)
    to_first = a[:rows, :BS] + a[rows:, :BS] + a[:rows, BS:]
    left = cat([cat([f_high, f_high], axis=1), cat([f_low, jnp.zeros_like(f_low)], axis=1)], axis=0)
    b = mb(left, stack, NN)
    return to_first, b[:rows] + b[rows:]


def start_kernel(wide, cap, own_blocks, pairs, points, q_in, unit, out, raw, q, vec, meta, sems, sem):
    vec_rows = q.shape[0]
    slot_rows = BS + vec_rows
    size = raw.shape[0] // CHUNKS
    loads = [
        pltpu.make_async_copy(
            points.at[pl.ds(k * size, size), :], raw.at[pl.ds(k * size, size), :], sems.at[k]
        )
        for k in range(CHUNKS)
    ]
    loads.append(pltpu.make_async_copy(q_in, q, sems.at[CHUNKS]))
    for load in loads:
        load.start()

    for k in range(CHUNKS):
        loads[k].wait()
        for b in range(own_blocks // CHUNKS):
            rows = pl.ds(k * size + b * BS, BS)
            x = raw[rows, :].astype(F32)
            x = x * lax.rsqrt(jnp.sum(x * x, axis=-1, keepdims=True) + EPSILON)
            unit[rows, :] = x.astype(BF)

    def send(p, carry):
        for c in range(cap):
            i = lax.rem(pairs[0, p * cap + c], own_blocks)
            pltpu.make_async_copy(
                unit.at[block(i), :], out.at[p, pl.ds(c * slot_rows, BS), :], sem
            ).start()
        return carry

    lax.fori_loop(0, wide, send, 0, unroll=4)
    loads[-1].wait()
    high, low = split(q[...])
    for b in range(own_blocks):
        cols = slice(b * BS, (b + 1) * BS)
        vec[b] = cat([high[:, cols], low[:, cols]], axis=1)
    both = cat([high, low], axis=0)
    gram = mb(both, both, NT)
    gram = gram[:vec_rows, :vec_rows] + (gram[:vec_rows, vec_rows:] + gram[vec_rows:, :vec_rows])
    pieces = []
    for _ in range(3):
        pieces.append(gram.astype(BF).astype(F32))
        gram = gram - pieces[-1]
    sums = cat(pieces + [jnp.zeros((vec_rows, BS - 3 * vec_rows), F32)], axis=1)
    lanes = lax.broadcasted_iota(jnp.int32, sums.shape, 1)

    def label(p, carry):
        ids = [lax.rem(pairs[1, p * cap + c], own_blocks).astype(F32) for c in range(cap)]
        left = jnp.where(lanes < BS // 2, sums, ids[0])
        meta[p] = cat([left, jnp.full(sums.shape, ids[1])], axis=1).astype(BF)
        for c in range(cap):
            i = lax.rem(pairs[0, p * cap + c], own_blocks)
            pltpu.make_async_copy(
                vec.at[i], out.at[p, pl.ds(c * slot_rows + BS, vec_rows), :], sem
            ).start()
        pltpu.make_async_copy(
            meta.at[p], out.at[p, pl.ds(cap * slot_rows, vec_rows), :], sem
        ).start()
        return carry

    lax.fori_loop(0, wide, label, 0, unroll=4)
    pltpu.make_async_copy(out, out, sem).wait()


def put_terms(terms, ids, first_slot, cap, rows, back, total):
    for s, (to_first, to_second) in enumerate(terms):
        back[(first_slot + s) // cap, (s % cap) * rows : (s % cap + 1) * rows, :] = to_first
        total[:, block(ids[s])] += to_second


def tiles_kernel(peers, cap, sent, unit, q, tiles, back, total, gram, ids, got, sems):
    wide = got.shape[0]
    vec_rows = q.shape[0]
    slot_rows = BS + vec_rows
    slots = range(peers * cap)

    def load(k):
        part = pl.ds(k * peers, peers)
        return pltpu.make_async_copy(sent.at[part], got.at[part], sems.at[k])

    for k in range(wide // peers):
        load(k).start()
    total[...] = jnp.zeros_like(total)
    gram[...] = jnp.zeros_like(gram)

    def chunk(k, carry):
        load(k).wait()
        peer = k * peers
        held = []
        for p in range(peers):
            label = got[peer + p, pl.ds(cap * slot_rows, vec_rows), :].astype(F32)
            gram[...] += label[:, :BS]
            for c in range(cap):
                j = label[0, (c + 1) * (BS // 2)].astype(jnp.int32)
                ids[(peer + p) * cap + c] = j
                held.append(j)
        stacks = []
        for s in slots:
            rows = pl.ds((s % cap) * slot_rows, BS)
            inner = mb(got[peer + s // cap, rows, :], unit[block(held[s]), :], NT)
            stacks.append(tile_stack(jnp.exp(KERNEL_FACTOR * (inner - 1.0))))
            tiles[peer * cap + s] = stacks[s]
        terms = []
        for s in slots:
            rows = pl.ds((s % cap) * slot_rows + BS, vec_rows)
            first = (got[peer + s // cap, rows, :BS], got[peer + s // cap, rows, BS:])
            terms.append(pair_terms(stacks[s], first, split(q[:, block(held[s])])))
        put_terms(terms, held, peer * cap, cap, vec_rows, back, total)
        return carry

    lax.fori_loop(0, wide // peers, chunk, 0)


def terms_kernel(peers, cap, ids, got, tiles, w0, back, total):
    vec_rows = w0.shape[0]
    slots = range(peers * cap)
    total[...] = jnp.zeros_like(total)

    def chunk(k, carry):
        peer = k * peers
        held = [ids[peer * cap + s] for s in slots]
        terms = []
        for s in slots:
            first = got[peer + s // cap, pl.ds((s % cap) * vec_rows, vec_rows), :]
            second = w0[:, block(held[s])]
            terms.append(pair_terms(tiles[peer * cap + s], split(first), split(second)))
        put_terms(terms, held, peer * cap, cap, vec_rows, back, total)
        return carry

    lax.fori_loop(0, got.shape[0] // peers, chunk, 0)


def sum_kernel(cap, own_blocks, pairs, got, total, out):
    vec_rows = total.shape[0]
    out[...] = total[...]

    def add(p, carry):
        for c in range(cap):
            i = lax.rem(pairs[0, p * cap + c], own_blocks)
            out[:, block(i)] += got[p, c * vec_rows : (c + 1) * vec_rows, :]
        return carry

    lax.fori_loop(0, got.shape[0], add, 0, unroll=4)


def first_factor_kernel(points, gram, matrix):
    g = gram[...]
    n = g.shape[0]
    _, inverse = factor_of((g[:, :n] + g[:, n : 2 * n] + g[:, 2 * n : 3 * n]) * (1.0 / points))
    none = jnp.zeros_like(inverse)
    matrix[...] = cat([cat([inverse, none], axis=1), cat([none, inverse], axis=1)], axis=0)


def factor_kernel(points, cap, last, got, matrix, along, low_out):
    n = along.shape[0]
    a, low, inverse, turned = step_matrices(got[:, cap * n :, :], points)
    along[...] = a
    low_out[...] = low
    none = jnp.zeros_like(low)
    across = mm(-low, (lax.broadcasted_iota(jnp.int32, (n, n), 0) == lax.broadcasted_iota(jnp.int32, (n, n), 1)).astype(F32), TN)
    lines = [cat([inverse, -turned, none, none], axis=1)]
    if not last:
        lines.append(cat([none, none, inverse, -turned], axis=1))
    lines.append(cat([none, across, inverse, -turned], axis=1))
    matrix[...] = cat(lines, axis=0)


def update_kernel(cap, own_blocks, old, pairs, t0, t1, t2, t3, *refs):
    given, matrix, outs, out = refs[:old], refs[old], refs[old + 1 : -1], refs[-1]
    image = (t0[...] + t2[...]) + (t1[...] + t3[...])
    rows = [r[...] for r in given]
    rows.insert(2 if old > 1 else 1, image)
    new = apply_small(matrix[...], cat(rows, axis=0))
    n = image.shape[0]
    for k, ref in enumerate(outs):
        ref[...] = new[k * n : (k + 1) * n]
    q, w0 = outs[0], outs[-1]
    tail = fold(new[:n], new[-n:])
    if not cap:
        out[...] = jnp.broadcast_to(tail[None], out.shape)
        return

    def put(p, carry):
        for c in range(cap):
            i = lax.rem(pairs[0, p * cap + c], own_blocks)
            out[p, c * n : (c + 1) * n, :] = w0[:, block(i)]
        out[p, cap * n :, :] = tail
        return carry

    lax.fori_loop(0, out.shape[0], put, 0, unroll=4)


def finish_kernel(points, got, w0, q, a0, l0, a1, l1, basis, coeffs):
    a, low, inverse, turned = step_matrices(got[...], points)
    basis[...] = apply_small(cat([inverse, -turned], axis=1), cat([w0[...], q[...]], axis=0))
    for k, m in enumerate((a0[...], l0[...], a1[...], l1[...], a, low)):
        coeffs[k // 2, k % 2] = m


def call(kernel, outs, n_ids=0, limit=VMEM_LIMIT, **more):
    params = pltpu.CompilerParams(vmem_limit_bytes=limit)
    shapes = tuple(jax.ShapeDtypeStruct(s, d) for s, d in outs)
    def run(*args):
        given = dict(more)
        vmem = pl.BlockSpec(memory_space=pltpu.VMEM)
        places = [pl.BlockSpec(memory_space=pltpu.SMEM)] * n_ids + [vmem] * (len(args) - n_ids)
        given.setdefault("in_specs", places)
        given.setdefault("out_specs", (vmem,) * len(outs))
        return pl.pallas_call(kernel, out_shape=shapes, compiler_params=params, **given)(*args)

    return run


def per_device(points, q_init, pairs):
    wide = lax.axis_size("wide")
    narrow = lax.axis_size("narrow")
    own_points, width = points.shape
    own_blocks = own_points // BS
    vec_rows = q_init.shape[0]
    pair_count = pairs.shape[1]
    cap = pair_count // wide
    total_points = own_points * wide
    slot_rows = BS + vec_rows
    start_rows = cap * slot_rows + vec_rows
    peers = min(8, wide)
    vectors = ((vec_rows, own_points), F32)
    small = ((vec_rows, vec_rows), F32)
    payload = ((wide, cap * vec_rows + TAIL, BS), F32)
    reply = ((wide, cap * vec_rows, BS), F32)
    tail = ((wide, TAIL, BS), F32)

    def exchange(x):
        return lax.all_to_all(x, "wide", split_axis=0, concat_axis=0, tiled=True)

    anywhere = pl.BlockSpec(memory_space=pl.ANY)
    unit, sent = call(
        functools.partial(start_kernel, wide, cap, own_blocks),
        [((own_points, width), BF), ((wide, start_rows, width), BF)],
        1,
        VMEM_START,
        in_specs=[pl.BlockSpec(memory_space=pltpu.SMEM), anywhere, anywhere],
        out_specs=(pl.BlockSpec(memory_space=pltpu.VMEM), anywhere),
        scratch_shapes=[
            pltpu.VMEM((own_points, width), BF),
            pltpu.VMEM((vec_rows, own_points), F32),
            pltpu.VMEM((own_blocks, vec_rows, 2 * BS), BF),
            pltpu.VMEM((wide, vec_rows, width), BF),
            pltpu.SemaphoreType.DMA((CHUNKS + 1,)),
            pltpu.SemaphoreType.DMA,
        ],
    )(pairs, points, q_init)
    vmem = pl.BlockSpec(memory_space=pltpu.VMEM)
    tiles, back, total, gram, ids = call(
        functools.partial(tiles_kernel, peers, cap),
        [
            ((pair_count, 2 * BS, BS), BF),
            reply,
            vectors,
            ((vec_rows, BS), F32),
            ((pair_count,), jnp.int32),
        ],
        0,
        VMEM_TILES,
        in_specs=[anywhere, vmem, vmem],
        out_specs=(vmem, vmem, vmem, vmem, pl.BlockSpec(memory_space=pltpu.SMEM)),
        scratch_shapes=[
            pltpu.VMEM((wide, start_rows, width), BF),
            pltpu.SemaphoreType.DMA((wide // peers,)),
        ],
    )(exchange(sent), unit, q_init)

    def narrow_terms(back, total):
        (total,) = call(functools.partial(sum_kernel, cap, own_blocks), [vectors], 1)(
            pairs, exchange(back), total
        )
        return (total,) + tuple(
            lax.ppermute(total, "narrow", [(i, (i + s) % narrow) for i in range(narrow)])
            for s in range(1, narrow)
        )

    sums = narrow_terms(back, total)
    (matrix,) = call(
        functools.partial(first_factor_kernel, total_points), [((2 * vec_rows, 2 * vec_rows), F32)]
    )(gram)
    q, w0, out = call(
        functools.partial(update_kernel, cap, own_blocks, 1), [vectors, vectors, payload], 1
    )(pairs, *sums, q_init, matrix)
    y = w0
    records = []
    for step in range(1, STEPS):
        last = step == STEPS - 1
        got = exchange(out)
        back, total = call(
            functools.partial(terms_kernel, 2 * peers, cap), [reply, vectors], 1
        )(ids, got, tiles, w0)
        sums = narrow_terms(back, total)
        count = 2 if last else 3
        matrix, along, low = call(
            functools.partial(factor_kernel, total_points, cap, last),
            [((count * vec_rows, 4 * vec_rows), F32), small, small],
        )(got)
        *new, out = call(
            functools.partial(update_kernel, 0 if last else cap, own_blocks, 3),
            [vectors] * count + [tail if last else payload],
            1,
        )(pairs, *sums, w0, q, y, matrix)
        q, y, w0 = new[0], new[1], new[-1]
        records += [along, low]
    return call(
        functools.partial(finish_kernel, total_points),
        [vectors, ((STEPS, 2, vec_rows, vec_rows), F32)],
    )(exchange(out), w0, q, *records)


def solution(mesh):
    placed = (P("wide", None), P(None, "wide"), P(None, ("wide", "narrow")))
    return jax.shard_map(
        per_device, mesh=mesh, in_specs=placed, out_specs=(P(None, "wide"), P()), check_vma=False
    )
```

```python
import functools

import jax
import jax.numpy as jnp
from jax import lax
from jax.experimental import pallas as pl
from jax.experimental.pallas import tpu as pltpu
from jax.sharding import PartitionSpec as P

BS = 128
STEPS = 3
KERNEL_FACTOR = 3.0
EPSILON = 1e-06
HIGH = lax.Precision.HIGHEST
VMEM_LIMIT = 16 * 2**20
VMEM_START = 60 * 2**20
VMEM_TILES = 30 * 2**20
TAIL = 8
CHUNKS = 8
BF = jnp.bfloat16
F32 = jnp.float32
NT = (((1,), (1,)), ((), ()))
TN = (((0,), (0,)), ((), ()))
NN = (((1,), (0,)), ((), ()))
cat = jnp.concatenate


def mm(a, b, dims):
    return lax.dot_general(a, b, dims, precision=HIGH, preferred_element_type=F32)


def mb(a, b, dims):
    return lax.dot_general(a, b, dims, preferred_element_type=F32)


def split(x):
    high = x.astype(BF)
    return high, (x - high.astype(F32)).astype(BF)


def block(i):
    return pl.ds(pl.multiple_of(i * BS, BS), BS)


def apply_small(m, x):
    rows = m.shape[0]
    m_high, m_low = split(m)
    left = cat([cat([m_high, m_high], axis=1), cat([m_low, jnp.zeros_like(m_low)], axis=1)], axis=0)
    out = mb(left, cat(split(x), axis=0), NN)
    return out[:rows] + out[rows:]


def factor_of(gram):
    n = gram.shape[0]
    rows = lax.broadcasted_iota(jnp.int32, (n, n), 0)
    cols = lax.broadcasted_iota(jnp.int32, (n, n), 1)
    same = (rows == cols).astype(F32)
    low, inverse, left = same, same, gram
    across, down = jnp.ones((1, n), F32), jnp.ones((n, 1), F32)
    for j in range(n):
        pivot = left[j : j + 1, j : j + 1]
        column = jnp.where(rows > j, left[:, j : j + 1] * (1.0 / pivot), 0.0)
        left = left - column * left[j : j + 1, :]
        inverse = inverse - column * inverse[j : j + 1, :]
        low = jnp.where(cols == j, low + column, low)
        across = jnp.where(cols[:1] == j, pivot, across)
        down = jnp.where(rows[:, :1] == j, pivot, down)
    return low * jnp.sqrt(across), inverse * (1.0 / jnp.sqrt(down))


def fold(q, w):
    n = q.shape[0]
    both = cat(split(cat([q, w], axis=0)), axis=0)
    g = mb(both, both, NT)
    g = g[: 2 * n, : 2 * n] + (g[: 2 * n, 2 * n :] + g[2 * n :, : 2 * n])
    parts = (g[:n, :n], g[:n, n:], g[n:, n:])
    pieces = [p[h : h + 8] for p in parts for h in (0, 8)]
    return cat(pieces + [jnp.zeros((8, BS - 6 * n), F32)], axis=1)


def step_matrices(tails, points):
    t = jnp.sum(tails, axis=0) * (1.0 / points)
    s, a, b = (cat([t[:, 32 * k : 32 * k + 16], t[:, 32 * k + 16 : 32 * k + 32]], axis=0) for k in range(3))
    g = b - mm(a, 2.0 * a - mm(s, a, NN), TN)
    low, inverse = factor_of(g)
    return a, low, inverse, mm(inverse, a, NT)


def tile_stack(tile):
    return cat(split(tile), axis=0)


def pair_terms(stack, first, second):
    f_high, f_low = first
    s_high, s_low = second
    rows = f_high.shape[0]
    a = mb(cat([s_high, s_low], axis=0), stack, NT)
    to_first = a[:rows, :BS] + a[rows:, :BS] + a[:rows, BS:]
    left = cat([cat([f_high, f_high], axis=1), cat([f_low, jnp.zeros_like(f_low)], axis=1)], axis=0)
    b = mb(left, stack, NN)
    return to_first, b[:rows] + b[rows:]


def start_kernel(wide, cap, own_blocks, pairs, points, q_in, unit_out, out, unit, raw, q, meta, sems, sem):
    vec_rows = q.shape[0]
    slot_rows = BS + vec_rows
    size = raw.shape[0] // CHUNKS
    loads = [
        pltpu.make_async_copy(
            points.at[pl.ds(k * size, size), :], raw.at[pl.ds(k * size, size), :], sems.at[k]
        )
        for k in range(CHUNKS)
    ]
    loads.append(pltpu.make_async_copy(q_in, q, sems.at[CHUNKS]))
    for load in (loads[-1], *loads[:-1]):
        load.start()
    loads[-1].wait()
    high, low = split(q[...])
    for b in range(own_blocks):
        cols = slice(b * BS, (b + 1) * BS)
        unit[b, BS:, :] = cat([high[:, cols], low[:, cols]], axis=1)
    half = own_blocks // 2
    for k in range(CHUNKS):
        loads[k].wait()
        for b in range(own_blocks // CHUNKS):
            x = raw[pl.ds(k * size + b * BS, BS), :].astype(F32)
            x = x * lax.rsqrt(jnp.sum(x * x, axis=-1, keepdims=True) + EPSILON)
            unit[k * (own_blocks // CHUNKS) + b, :BS, :] = x.astype(BF)
        if k % (CHUNKS // 2) != CHUNKS // 2 - 1:
            continue
        late = k == CHUNKS - 1

        def send(p, carry, late=late):
            for c in range(cap):
                i = lax.rem(pairs[0, p * cap + c], own_blocks)

                @pl.when((i >= half) == late)
                def _(i=i, c=c):
                    pltpu.make_async_copy(
                        unit.at[i], out.at[p, pl.ds(c * slot_rows, slot_rows), :], sem
                    ).start()

            return carry

        lax.fori_loop(0, wide, send, 0, unroll=8)
    keep = pltpu.make_async_copy(unit, unit_out, sems.at[CHUNKS + 1])
    keep.start()
    both = cat([high, low], axis=0)
    gram = mb(both, both, NT)
    gram = gram[:vec_rows, :vec_rows] + (gram[:vec_rows, vec_rows:] + gram[vec_rows:, :vec_rows])
    pieces = []
    for _ in range(3):
        pieces.append(gram.astype(BF).astype(F32))
        gram = gram - pieces[-1]
    sums = cat(pieces + [jnp.zeros((vec_rows, BS - 3 * vec_rows), F32)], axis=1)
    lanes = lax.broadcasted_iota(jnp.int32, sums.shape, 1)

    def label(p, carry):
        ids = [lax.rem(pairs[1, p * cap + c], own_blocks).astype(F32) for c in range(cap)]
        left = jnp.where(lanes < BS // 2, sums, ids[0])
        meta[p] = cat([left, jnp.full(sums.shape, ids[1])], axis=1).astype(BF)
        return carry

    lax.fori_loop(0, wide, label, 0, unroll=8)
    pltpu.make_async_copy(meta, out.at[:, pl.ds(cap * slot_rows, vec_rows), :], sem).start()
    pltpu.make_async_copy(out, out, sem).wait()
    keep.wait()


def put_terms(terms, ids, first_slot, cap, rows, back, total):
    for s, (to_first, to_second) in enumerate(terms):
        back[(first_slot + s) // cap, (s % cap) * rows : (s % cap + 1) * rows, :] = to_first
        total[:, block(ids[s])] += to_second


def tiles_kernel(peers, cap, sent, unit, q, tiles, back, total, gram, ids, got, labels, sems):
    wide = got.shape[0]
    vec_rows = q.shape[0]
    slot_rows = BS + vec_rows
    slots = range(peers * cap)
    steps = wide // peers

    def load(k):
        part = pl.ds(k * peers, peers)
        here = pl.ds(0, cap * slot_rows)
        return pltpu.make_async_copy(sent.at[part, here], got.at[part], sems.at[k])

    first = pltpu.make_async_copy(
        sent.at[:, pl.ds(cap * slot_rows, vec_rows)], labels, sems.at[steps]
    )
    first.start()
    for k in range(steps):
        load(k).start()
    total[...] = jnp.zeros_like(total)
    first.wait()
    gram[...] = jnp.sum(labels[:, :, :BS].astype(F32), axis=0)
    for p in range(wide):
        label = labels[p].astype(F32)
        for c in range(cap):
            ids[p * cap + c] = label[0, (c + 1) * (BS // 2)].astype(jnp.int32)

    def chunk(k, carry):
        load(k).wait()
        peer = k * peers
        held = [ids[peer * cap + s] for s in slots]
        stacks = []
        for s in slots:
            rows = pl.ds((s % cap) * slot_rows, BS)
            inner = mb(got[peer + s // cap, rows, :], unit[held[s], :BS, :], NT)
            stacks.append(tile_stack(jnp.exp(KERNEL_FACTOR * (inner - 1.0))))
            tiles[peer * cap + s] = stacks[s]
        terms = []
        for s in slots:
            rows = pl.ds((s % cap) * slot_rows + BS, vec_rows)
            first = (got[peer + s // cap, rows, :BS], got[peer + s // cap, rows, BS:])
            terms.append(pair_terms(stacks[s], first, split(q[:, block(held[s])])))
        put_terms(terms, held, peer * cap, cap, vec_rows, back, total)
        return carry

    lax.fori_loop(0, steps, chunk, 0)


def terms_kernel(peers, cap, ids, got, tiles, w0, back, total):
    vec_rows = w0.shape[0]
    slots = range(peers * cap)
    total[...] = jnp.zeros_like(total)

    def chunk(k, carry):
        peer = k * peers
        held = [ids[peer * cap + s] for s in slots]
        terms = []
        for s in slots:
            first = got[peer + s // cap, pl.ds((s % cap) * vec_rows, vec_rows), :]
            second = w0[:, block(held[s])]
            terms.append(pair_terms(tiles[peer * cap + s], split(first), split(second)))
        put_terms(terms, held, peer * cap, cap, vec_rows, back, total)
        return carry

    lax.fori_loop(0, got.shape[0] // peers, chunk, 0)


def sum_kernel(cap, own_blocks, pairs, got, total, out):
    vec_rows = total.shape[0]
    out[...] = total[...]

    def add(p, carry):
        for c in range(cap):
            i = lax.rem(pairs[0, p * cap + c], own_blocks)
            out[:, block(i)] += got[p, c * vec_rows : (c + 1) * vec_rows, :]
        return carry

    lax.fori_loop(0, got.shape[0], add, 0, unroll=8)


def first_factor_kernel(points, gram, matrix):
    g = gram[...]
    n = g.shape[0]
    _, inverse = factor_of((g[:, :n] + g[:, n : 2 * n] + g[:, 2 * n : 3 * n]) * (1.0 / points))
    none = jnp.zeros_like(inverse)
    matrix[...] = cat([cat([inverse, none], axis=1), cat([none, inverse], axis=1)], axis=0)


def factor_kernel(points, cap, last, got, matrix, along, low_out):
    n = along.shape[0]
    a, low, inverse, turned = step_matrices(got[:, cap * n :, :], points)
    along[...] = a
    low_out[...] = low
    none = jnp.zeros_like(low)
    across = mm(-low, (lax.broadcasted_iota(jnp.int32, (n, n), 0) == lax.broadcasted_iota(jnp.int32, (n, n), 1)).astype(F32), TN)
    lines = [cat([inverse, -turned, none, none], axis=1)]
    if not last:
        lines.append(cat([none, none, inverse, -turned], axis=1))
    lines.append(cat([none, across, inverse, -turned], axis=1))
    matrix[...] = cat(lines, axis=0)


def update_kernel(cap, own_blocks, old, pairs, t0, t1, t2, t3, *refs):
    given, matrix, outs, out = refs[:old], refs[old], refs[old + 1 : -1], refs[-1]
    image = (t0[...] + t2[...]) + (t1[...] + t3[...])
    rows = [r[...] for r in given]
    rows.insert(2 if old > 1 else 1, image)
    new = apply_small(matrix[...], cat(rows, axis=0))
    n = image.shape[0]
    for k, ref in enumerate(outs):
        ref[...] = new[k * n : (k + 1) * n]
    q, w0 = outs[0], outs[-1]
    tail = fold(new[:n], new[-n:])
    if not cap:
        out[...] = jnp.broadcast_to(tail[None], out.shape)
        return

    def put(p, carry):
        for c in range(cap):
            i = lax.rem(pairs[0, p * cap + c], own_blocks)
            out[p, c * n : (c + 1) * n, :] = w0[:, block(i)]
        out[p, cap * n :, :] = tail
        return carry

    lax.fori_loop(0, out.shape[0], put, 0, unroll=8)


def finish_kernel(points, got, w0, q, a0, l0, a1, l1, basis, coeffs):
    a, low, inverse, turned = step_matrices(got[...], points)
    basis[...] = apply_small(cat([inverse, -turned], axis=1), cat([w0[...], q[...]], axis=0))
    for k, m in enumerate((a0[...], l0[...], a1[...], l1[...], a, low)):
        coeffs[k // 2, k % 2] = m


def call(kernel, outs, n_ids=0, limit=VMEM_LIMIT, **more):
    params = pltpu.CompilerParams(vmem_limit_bytes=limit)
    shapes = tuple(jax.ShapeDtypeStruct(s, d) for s, d in outs)
    def run(*args):
        given = dict(more)
        vmem = pl.BlockSpec(memory_space=pltpu.VMEM)
        places = [pl.BlockSpec(memory_space=pltpu.SMEM)] * n_ids + [vmem] * (len(args) - n_ids)
        given.setdefault("in_specs", places)
        given.setdefault("out_specs", (vmem,) * len(outs))
        return pl.pallas_call(kernel, out_shape=shapes, compiler_params=params, **given)(*args)

    return run


def per_device(points, q_init, pairs):
    wide = lax.axis_size("wide")
    narrow = lax.axis_size("narrow")
    own_points, width = points.shape
    own_blocks = own_points // BS
    vec_rows = q_init.shape[0]
    pair_count = pairs.shape[1]
    cap = pair_count // wide
    total_points = own_points * wide
    slot_rows = BS + vec_rows
    start_rows = cap * slot_rows + vec_rows
    peers = min(8, wide)
    vectors = ((vec_rows, own_points), F32)
    small = ((vec_rows, vec_rows), F32)
    payload = ((wide, cap * vec_rows + TAIL, BS), F32)
    reply = ((wide, cap * vec_rows, BS), F32)
    tail = ((wide, TAIL, BS), F32)

    def exchange(x):
        return lax.all_to_all(x, "wide", split_axis=0, concat_axis=0, tiled=True)

    anywhere = pl.BlockSpec(memory_space=pl.ANY)
    unit, sent = call(
        functools.partial(start_kernel, wide, cap, own_blocks),
        [((own_blocks, slot_rows, width), BF), ((wide, start_rows, width), BF)],
        1,
        VMEM_START,
        in_specs=[pl.BlockSpec(memory_space=pltpu.SMEM), anywhere, anywhere],
        out_specs=(anywhere, anywhere),
        scratch_shapes=[
            pltpu.VMEM((own_blocks, slot_rows, width), BF),
            pltpu.VMEM((own_points, width), BF),
            pltpu.VMEM((vec_rows, own_points), F32),
            pltpu.VMEM((wide, vec_rows, width), BF),
            pltpu.SemaphoreType.DMA((CHUNKS + 2,)),
            pltpu.SemaphoreType.DMA,
        ],
    )(pairs, points, q_init)
    vmem = pl.BlockSpec(memory_space=pltpu.VMEM)
    tiles, back, total, gram, ids = call(
        functools.partial(tiles_kernel, peers * 2, cap),
        [
            ((pair_count, 2 * BS, BS), BF),
            reply,
            vectors,
            ((vec_rows, BS), F32),
            ((pair_count,), jnp.int32),
        ],
        0,
        VMEM_TILES,
        in_specs=[anywhere, vmem, vmem],
        out_specs=(vmem, vmem, vmem, vmem, pl.BlockSpec(memory_space=pltpu.SMEM)),
        scratch_shapes=[
            pltpu.VMEM((wide, cap * slot_rows, width), BF),
            pltpu.VMEM((wide, vec_rows, width), BF),
            pltpu.SemaphoreType.DMA((wide // peers + 1,)),
        ],
    )(exchange(sent), unit, q_init)

    def narrow_terms(back, total):
        (total,) = call(functools.partial(sum_kernel, cap, own_blocks), [vectors], 1)(
            pairs, exchange(back), total
        )
        return (total,) + tuple(
            lax.ppermute(total, "narrow", [(i, (i + s) % narrow) for i in range(narrow)])
            for s in range(1, narrow)
        )

    sums = narrow_terms(back, total)
    (matrix,) = call(
        functools.partial(first_factor_kernel, total_points), [((2 * vec_rows, 2 * vec_rows), F32)]
    )(gram)
    q, w0, out = call(
        functools.partial(update_kernel, cap, own_blocks, 1), [vectors, vectors, payload], 1
    )(pairs, *sums, q_init, matrix)
    y = w0
    records = []
    for step in range(1, STEPS):
        last = step == STEPS - 1
        got = exchange(out)
        back, total = call(
            functools.partial(terms_kernel, 4 * peers, cap), [reply, vectors], 1
        )(ids, got, tiles, w0)
        sums = narrow_terms(back, total)
        count = 2 if last else 3
        matrix, along, low = call(
            functools.partial(factor_kernel, total_points, cap, last),
            [((count * vec_rows, 4 * vec_rows), F32), small, small],
        )(got)
        *new, out = call(
            functools.partial(update_kernel, 0 if last else cap, own_blocks, 3),
            [vectors] * count + [tail if last else payload],
            1,
        )(pairs, *sums, w0, q, y, matrix)
        q, y, w0 = new[0], new[1], new[-1]
        records += [along, low]
    return call(
        functools.partial(finish_kernel, total_points),
        [vectors, ((STEPS, 2, vec_rows, vec_rows), F32)],
    )(exchange(out), w0, q, *records)


def solution(mesh):
    placed = (P("wide", None), P(None, "wide"), P(None, ("wide", "narrow")))
    return jax.shard_map(
        per_device, mesh=mesh, in_specs=placed, out_specs=(P(None, "wide"), P()), check_vma=False
    )
```

```python
import functools

import jax
import jax.numpy as jnp
from jax import lax
from jax.experimental import pallas as pl
from jax.experimental.pallas import tpu as pltpu
from jax.sharding import PartitionSpec as P

BS = 128
STEPS = 3
KERNEL_FACTOR = 3.0
EPSILON = 1e-06
HIGH = lax.Precision.HIGHEST
VMEM_LIMIT = 16 * 2**20
VMEM_START = 60 * 2**20
VMEM_TILES = 30 * 2**20
TAIL = 8
CHUNKS = 8
BF = jnp.bfloat16
F32 = jnp.float32
NT = (((1,), (1,)), ((), ()))
TN = (((0,), (0,)), ((), ()))
NN = (((1,), (0,)), ((), ()))
cat = jnp.concatenate


def mm(a, b, dims):
    return lax.dot_general(a, b, dims, precision=HIGH, preferred_element_type=F32)


def mb(a, b, dims):
    return lax.dot_general(a, b, dims, preferred_element_type=F32)


def split(x):
    high = x.astype(BF)
    return high, (x - high.astype(F32)).astype(BF)


def block(i):
    return pl.ds(pl.multiple_of(i * BS, BS), BS)


def apply_small(m, x):
    rows = m.shape[0]
    m_high, m_low = split(m)
    left = cat([cat([m_high, m_high], axis=1), cat([m_low, jnp.zeros_like(m_low)], axis=1)], axis=0)
    out = mb(left, cat(split(x), axis=0), NN)
    return out[:rows] + out[rows:]


def factor_of(gram):
    n = gram.shape[0]
    rows = lax.broadcasted_iota(jnp.int32, (n, n), 0)
    cols = lax.broadcasted_iota(jnp.int32, (n, n), 1)
    same = (rows == cols).astype(F32)
    low, inverse, left = same, same, gram
    across, down = jnp.ones((1, n), F32), jnp.ones((n, 1), F32)
    for j in range(n):
        pivot = left[j : j + 1, j : j + 1]
        column = jnp.where(rows > j, left[:, j : j + 1] * (1.0 / pivot), 0.0)
        left = left - column * left[j : j + 1, :]
        inverse = inverse - column * inverse[j : j + 1, :]
        low = jnp.where(cols == j, low + column, low)
        across = jnp.where(cols[:1] == j, pivot, across)
        down = jnp.where(rows[:, :1] == j, pivot, down)
    return low * jnp.sqrt(across), inverse * (1.0 / jnp.sqrt(down))


def fold(q, w):
    n = q.shape[0]
    both = cat(split(cat([q, w], axis=0)), axis=0)
    g = mb(both, both, NT)
    g = g[: 2 * n, : 2 * n] + (g[: 2 * n, 2 * n :] + g[2 * n :, : 2 * n])
    parts = (g[:n, :n], g[:n, n:], g[n:, n:])
    pieces = [p[h : h + 8] for p in parts for h in (0, 8)]
    return cat(pieces + [jnp.zeros((8, BS - 6 * n), F32)], axis=1)


def step_matrices(tails, points):
    t = jnp.sum(tails, axis=0) * (1.0 / points)
    s, a, b = (cat([t[:, 32 * k : 32 * k + 16], t[:, 32 * k + 16 : 32 * k + 32]], axis=0) for k in range(3))
    g = b - mm(a, 2.0 * a - mm(s, a, NN), TN)
    low, inverse = factor_of(g)
    return a, low, inverse, mm(inverse, a, NT)


def tile_stack(tile):
    return cat(split(tile), axis=0)


def pair_terms(stack, first, second):
    f_high, f_low = first
    s_high, s_low = second
    rows = f_high.shape[0]
    a = mb(cat([s_high, s_low], axis=0), stack, NT)
    to_first = a[:rows, :BS] + a[rows:, :BS] + a[:rows, BS:]
    left = cat([cat([f_high, f_high], axis=1), cat([f_low, jnp.zeros_like(f_low)], axis=1)], axis=0)
    b = mb(left, stack, NN)
    return to_first, b[:rows] + b[rows:]


def start_kernel(wide, cap, own_blocks, pairs, points, q_in, unit_out, out, unit, raw, q, meta, sems, sem):
    vec_rows = q.shape[0]
    slot_rows = BS + vec_rows
    size = raw.shape[0] // CHUNKS
    loads = [
        pltpu.make_async_copy(
            points.at[pl.ds(k * size, size), :], raw.at[pl.ds(k * size, size), :], sems.at[k]
        )
        for k in range(CHUNKS)
    ]
    loads.append(pltpu.make_async_copy(q_in, q, sems.at[CHUNKS]))
    for load in (loads[-1], *loads[:-1]):
        load.start()
    loads[-1].wait()
    high, low = split(q[...])
    for b in range(own_blocks):
        cols = slice(b * BS, (b + 1) * BS)
        unit[b, BS:, :] = cat([high[:, cols], low[:, cols]], axis=1)
    half = own_blocks // 2
    for k in range(CHUNKS):
        loads[k].wait()
        for b in range(own_blocks // CHUNKS):
            x = raw[pl.ds(k * size + b * BS, BS), :].astype(F32)
            x = x * lax.rsqrt(jnp.sum(x * x, axis=-1, keepdims=True) + EPSILON)
            unit[k * (own_blocks // CHUNKS) + b, :BS, :] = x.astype(BF)
        if k % (CHUNKS // 2) != CHUNKS // 2 - 1:
            continue
        late = k == CHUNKS - 1

        def send(p, carry, late=late):
            for c in range(cap):
                i = lax.rem(pairs[0, p * cap + c], own_blocks)

                @pl.when((i >= half) == late)
                def _(i=i, c=c):
                    pltpu.make_async_copy(
                        unit.at[i], out.at[p, pl.ds(c * slot_rows, slot_rows), :], sem
                    ).start()

            return carry

        lax.fori_loop(0, wide, send, 0, unroll=8)
    keep = pltpu.make_async_copy(unit, unit_out, sems.at[CHUNKS + 1])
    keep.start()
    both = cat([high, low], axis=0)
    gram = mb(both, both, NT)
    gram = gram[:vec_rows, :vec_rows] + (gram[:vec_rows, vec_rows:] + gram[vec_rows:, :vec_rows])
    pieces = []
    for _ in range(3):
        pieces.append(gram.astype(BF).astype(F32))
        gram = gram - pieces[-1]
    sums = cat(pieces + [jnp.zeros((vec_rows, BS - 3 * vec_rows), F32)], axis=1)
    lanes = lax.broadcasted_iota(jnp.int32, sums.shape, 1)

    def label(p, carry):
        ids = [lax.rem(pairs[1, p * cap + c], own_blocks).astype(F32) for c in range(cap)]
        left = jnp.where(lanes < BS // 2, sums, ids[0])
        meta[p] = cat([left, jnp.full(sums.shape, ids[1])], axis=1).astype(BF)
        return carry

    lax.fori_loop(0, wide, label, 0, unroll=8)
    pltpu.make_async_copy(meta, out.at[:, pl.ds(cap * slot_rows, vec_rows), :], sem).start()
    pltpu.make_async_copy(out, out, sem).wait()
    keep.wait()


def put_terms(terms, ids, first_slot, cap, rows, back, total):
    for s, (to_first, to_second) in enumerate(terms):
        back[(first_slot + s) // cap, (s % cap) * rows : (s % cap + 1) * rows, :] = to_first
        total[:, block(ids[s])] += to_second


def tiles_kernel(peers, cap, sent, unit, q, tiles, back, total, gram, ids, got, labels, sems):
    wide = got.shape[0]
    vec_rows = q.shape[0]
    slot_rows = BS + vec_rows
    slots = range(peers * cap)
    steps = wide // peers

    def load(k):
        part = pl.ds(k * peers, peers)
        here = pl.ds(0, cap * slot_rows)
        return pltpu.make_async_copy(sent.at[part, here], got.at[part], sems.at[k])

    first = pltpu.make_async_copy(
        sent.at[:, pl.ds(cap * slot_rows, vec_rows)], labels, sems.at[steps]
    )
    first.start()
    for k in range(steps):
        load(k).start()
    total[...] = jnp.zeros_like(total)
    first.wait()
    gram[...] = jnp.sum(labels[:, :, :BS].astype(F32), axis=0)
    for p in range(wide):
        label = labels[p].astype(F32)
        for c in range(cap):
            ids[p * cap + c] = label[0, (c + 1) * (BS // 2)].astype(jnp.int32)

    def chunk(k, carry):
        load(k).wait()
        peer = k * peers
        held = [ids[peer * cap + s] for s in slots]
        stacks = []
        for s in slots:
            rows = pl.ds((s % cap) * slot_rows, BS)
            inner = mb(got[peer + s // cap, rows, :], unit[held[s], :BS, :], NT)
            stacks.append(tile_stack(jnp.exp(KERNEL_FACTOR * (inner - 1.0))))
            tiles[peer * cap + s] = stacks[s]
        terms = []
        for s in slots:
            rows = pl.ds((s % cap) * slot_rows + BS, vec_rows)
            first = (got[peer + s // cap, rows, :BS], got[peer + s // cap, rows, BS:])
            terms.append(pair_terms(stacks[s], first, split(q[:, block(held[s])])))
        put_terms(terms, held, peer * cap, cap, vec_rows, back, total)
        return carry

    lax.fori_loop(0, steps, chunk, 0)


def terms_kernel(peers, cap, ids, got, tiles, w0, back, total):
    vec_rows = w0.shape[0]
    slots = range(peers * cap)
    total[...] = jnp.zeros_like(total)

    def chunk(k, carry):
        peer = k * peers
        held = [ids[peer * cap + s] for s in slots]
        terms = []
        for s in slots:
            first = got[peer + s // cap, pl.ds((s % cap) * vec_rows, vec_rows), :]
            second = w0[:, block(held[s])]
            terms.append(pair_terms(tiles[peer * cap + s], split(first), split(second)))
        put_terms(terms, held, peer * cap, cap, vec_rows, back, total)
        return carry

    lax.fori_loop(0, got.shape[0] // peers, chunk, 0)


def sum_kernel(cap, own_blocks, pairs, got, total, top, low):
    vec_rows = total.shape[0]
    half = vec_rows // 2
    top[...] = total[:half]
    low[...] = total[half:]

    def add(p, carry):
        for c in range(cap):
            i = lax.rem(pairs[0, p * cap + c], own_blocks)
            top[:, block(i)] += got[p, c * vec_rows : c * vec_rows + half, :]
            low[:, block(i)] += got[p, c * vec_rows + half : (c + 1) * vec_rows, :]
        return carry

    lax.fori_loop(0, got.shape[0], add, 0, unroll=8)


def first_factor_kernel(points, gram, matrix):
    g = gram[...]
    n = g.shape[0]
    _, inverse = factor_of((g[:, :n] + g[:, n : 2 * n] + g[:, 2 * n : 3 * n]) * (1.0 / points))
    none = jnp.zeros_like(inverse)
    matrix[...] = cat([cat([inverse, none], axis=1), cat([none, inverse], axis=1)], axis=0)


def factor_kernel(points, cap, last, got, matrix, along, low_out):
    n = along.shape[0]
    a, low, inverse, turned = step_matrices(got[:, cap * n :, :], points)
    along[...] = a
    low_out[...] = low
    none = jnp.zeros_like(low)
    across = mm(-low, (lax.broadcasted_iota(jnp.int32, (n, n), 0) == lax.broadcasted_iota(jnp.int32, (n, n), 1)).astype(F32), TN)
    lines = [cat([inverse, -turned, none, none], axis=1)]
    if not last:
        lines.append(cat([none, none, inverse, -turned], axis=1))
    lines.append(cat([none, across, inverse, -turned], axis=1))
    matrix[...] = cat(lines, axis=0)


def update_kernel(cap, own_blocks, old, pairs, t0, t1, b0, b1, *refs):
    given, matrix, outs, out = refs[:old], refs[old], refs[old + 1 : -1], refs[-1]
    image = cat([t0[...] + t1[...], b0[...] + b1[...]], axis=0)
    rows = [r[...] for r in given]
    rows.insert(2 if old > 1 else 1, image)
    new = apply_small(matrix[...], cat(rows, axis=0))
    n = image.shape[0]
    for k, ref in enumerate(outs):
        ref[...] = new[k * n : (k + 1) * n]
    q, w0 = outs[0], outs[-1]
    tail = fold(new[:n], new[-n:])
    if not cap:
        out[...] = jnp.broadcast_to(tail[None], out.shape)
        return

    def put(p, carry):
        for c in range(cap):
            i = lax.rem(pairs[0, p * cap + c], own_blocks)
            out[p, c * n : (c + 1) * n, :] = w0[:, block(i)]
        out[p, cap * n :, :] = tail
        return carry

    lax.fori_loop(0, out.shape[0], put, 0, unroll=8)


def finish_kernel(points, got, w0, q, a0, l0, a1, l1, basis, coeffs):
    a, low, inverse, turned = step_matrices(got[...], points)
    basis[...] = apply_small(cat([inverse, -turned], axis=1), cat([w0[...], q[...]], axis=0))
    for k, m in enumerate((a0[...], l0[...], a1[...], l1[...], a, low)):
        coeffs[k // 2, k % 2] = m


def call(kernel, outs, n_ids=0, limit=VMEM_LIMIT, **more):
    params = pltpu.CompilerParams(vmem_limit_bytes=limit)
    shapes = tuple(jax.ShapeDtypeStruct(s, d) for s, d in outs)
    def run(*args):
        given = dict(more)
        vmem = pl.BlockSpec(memory_space=pltpu.VMEM)
        places = [pl.BlockSpec(memory_space=pltpu.SMEM)] * n_ids + [vmem] * (len(args) - n_ids)
        given.setdefault("in_specs", places)
        given.setdefault("out_specs", (vmem,) * len(outs))
        return pl.pallas_call(kernel, out_shape=shapes, compiler_params=params, **given)(*args)

    return run


def per_device(points, q_init, pairs):
    wide = lax.axis_size("wide")
    narrow = lax.axis_size("narrow")
    own_points, width = points.shape
    own_blocks = own_points // BS
    vec_rows = q_init.shape[0]
    pair_count = pairs.shape[1]
    cap = pair_count // wide
    total_points = own_points * wide
    slot_rows = BS + vec_rows
    start_rows = cap * slot_rows + vec_rows
    peers = min(8, wide)
    vectors = ((vec_rows, own_points), F32)
    small = ((vec_rows, vec_rows), F32)
    payload = ((wide, cap * vec_rows + TAIL, BS), F32)
    reply = ((wide, cap * vec_rows, BS), F32)
    tail = ((wide, TAIL, BS), F32)

    def exchange(x):
        return lax.all_to_all(x, "wide", split_axis=0, concat_axis=0, tiled=True)

    anywhere = pl.BlockSpec(memory_space=pl.ANY)
    unit, sent = call(
        functools.partial(start_kernel, wide, cap, own_blocks),
        [((own_blocks, slot_rows, width), BF), ((wide, start_rows, width), BF)],
        1,
        VMEM_START,
        in_specs=[pl.BlockSpec(memory_space=pltpu.SMEM), anywhere, anywhere],
        out_specs=(anywhere, anywhere),
        scratch_shapes=[
            pltpu.VMEM((own_blocks, slot_rows, width), BF),
            pltpu.VMEM((own_points, width), BF),
            pltpu.VMEM((vec_rows, own_points), F32),
            pltpu.VMEM((wide, vec_rows, width), BF),
            pltpu.SemaphoreType.DMA((CHUNKS + 2,)),
            pltpu.SemaphoreType.DMA,
        ],
    )(pairs, points, q_init)
    vmem = pl.BlockSpec(memory_space=pltpu.VMEM)
    tiles, back, total, gram, ids = call(
        functools.partial(tiles_kernel, peers * 2, cap),
        [
            ((pair_count, 2 * BS, BS), BF),
            reply,
            vectors,
            ((vec_rows, BS), F32),
            ((pair_count,), jnp.int32),
        ],
        0,
        VMEM_TILES,
        in_specs=[anywhere, vmem, vmem],
        out_specs=(vmem, vmem, vmem, vmem, pl.BlockSpec(memory_space=pltpu.SMEM)),
        scratch_shapes=[
            pltpu.VMEM((wide, cap * slot_rows, width), BF),
            pltpu.VMEM((wide, vec_rows, width), BF),
            pltpu.SemaphoreType.DMA((wide // peers + 1,)),
        ],
    )(exchange(sent), unit, q_init)

    def swap(x, mask):
        return lax.ppermute(x, "narrow", [(i, i ^ mask) for i in range(narrow)])

    half = ((vec_rows // 2, own_points), F32)

    def narrow_terms(back, total):
        top, low = call(functools.partial(sum_kernel, cap, own_blocks), [half, half], 1)(
            pairs, exchange(back), total
        )
        top_from, low_from = swap(top, 1), swap(low, 3)
        top, low = top + top_from, low + low_from
        return top, swap(top, 3), low, swap(low, 1)

    sums = narrow_terms(back, total)
    (matrix,) = call(
        functools.partial(first_factor_kernel, total_points), [((2 * vec_rows, 2 * vec_rows), F32)]
    )(gram)
    q, w0, out = call(
        functools.partial(update_kernel, cap, own_blocks, 1), [vectors, vectors, payload], 1
    )(pairs, *sums, q_init, matrix)
    y = w0
    records = []
    for step in range(1, STEPS):
        last = step == STEPS - 1
        got = exchange(out)
        back, total = call(
            functools.partial(terms_kernel, 4 * peers, cap), [reply, vectors], 1
        )(ids, got, tiles, w0)
        sums = narrow_terms(back, total)
        count = 2 if last else 3
        matrix, along, low = call(
            functools.partial(factor_kernel, total_points, cap, last),
            [((count * vec_rows, 4 * vec_rows), F32), small, small],
        )(got)
        *new, out = call(
            functools.partial(update_kernel, 0 if last else cap, own_blocks, 3),
            [vectors] * count + [tail if last else payload],
            1,
        )(pairs, *sums, w0, q, y, matrix)
        q, y, w0 = new[0], new[1], new[-1]
        records += [along, low]
    return call(
        functools.partial(finish_kernel, total_points),
        [vectors, ((STEPS, 2, vec_rows, vec_rows), F32)],
    )(exchange(out), w0, q, *records)


def solution(mesh):
    placed = (P("wide", None), P(None, "wide"), P(None, ("wide", "narrow")))
    return jax.shard_map(
        per_device, mesh=mesh, in_specs=placed, out_specs=(P(None, "wide"), P()), check_vma=False
    )
```

```python
import functools

import jax
import jax.numpy as jnp
from jax import lax
from jax.experimental import pallas as pl
from jax.experimental.pallas import tpu as pltpu
from jax.sharding import PartitionSpec as P

BS = 128
STEPS = 3
KERNEL_FACTOR = 3.0
EPSILON = 1e-06
HIGH = lax.Precision.HIGHEST
VMEM_LIMIT = 16 * 2**20
VMEM_START = 60 * 2**20
VMEM_TILES = 30 * 2**20
TAIL = 8
CHUNKS = 8
BF = jnp.bfloat16
F32 = jnp.float32
NT = (((1,), (1,)), ((), ()))
TN = (((0,), (0,)), ((), ()))
NN = (((1,), (0,)), ((), ()))
cat = jnp.concatenate


def mm(a, b, dims):
    return lax.dot_general(a, b, dims, precision=HIGH, preferred_element_type=F32)


def mb(a, b, dims):
    return lax.dot_general(a, b, dims, preferred_element_type=F32)


def split(x):
    high = x.astype(BF)
    return high, (x - high.astype(F32)).astype(BF)


def block(i):
    return pl.ds(pl.multiple_of(i * BS, BS), BS)


def apply_small(m, x):
    rows = m.shape[0]
    m_high, m_low = split(m)
    left = cat([cat([m_high, m_high], axis=1), cat([m_low, jnp.zeros_like(m_low)], axis=1)], axis=0)
    out = mb(left, cat(split(x), axis=0), NN)
    return out[:rows] + out[rows:]


def factor_of(gram):
    n = gram.shape[0]
    rows = lax.broadcasted_iota(jnp.int32, (n, n), 0)
    cols = lax.broadcasted_iota(jnp.int32, (n, n), 1)
    same = (rows == cols).astype(F32)
    low, inverse, left = same, same, gram
    across, down = jnp.ones((1, n), F32), jnp.ones((n, 1), F32)
    for j in range(n):
        pivot = left[j : j + 1, j : j + 1]
        column = jnp.where(rows > j, left[:, j : j + 1] * (1.0 / pivot), 0.0)
        left = left - column * left[j : j + 1, :]
        inverse = inverse - column * inverse[j : j + 1, :]
        low = jnp.where(cols == j, low + column, low)
        across = jnp.where(cols[:1] == j, pivot, across)
        down = jnp.where(rows[:, :1] == j, pivot, down)
    return low * jnp.sqrt(across), inverse * (1.0 / jnp.sqrt(down))


def fold(q, w):
    n = q.shape[0]
    both = cat(split(cat([q, w], axis=0)), axis=0)
    g = mb(both, both, NT)
    g = g[: 2 * n, : 2 * n] + (g[: 2 * n, 2 * n :] + g[2 * n :, : 2 * n])
    parts = (g[:n, :n], g[:n, n:], g[n:, n:])
    pieces = [p[h : h + 8] for p in parts for h in (0, 8)]
    return cat(pieces + [jnp.zeros((8, BS - 6 * n), F32)], axis=1)


def sums_of(tails, points):
    t = jnp.sum(tails, axis=0) * (1.0 / points)
    return (cat([t[:, k : k + 16], t[:, k + 16 : k + 32]], axis=0) for k in (0, 32, 64))


def rest_gram(s, a, b):
    return b - mm(a, 2.0 * a - mm(s, a, NN), TN)


def step_matrices(tails, points):
    s, a, b = sums_of(tails, points)
    low, inverse = factor_of(rest_gram(s, a, b))
    return a, low, inverse, mm(inverse, a, NT)


def tile_stack(tile):
    return cat(split(tile), axis=0)


def first_term(stack, second):
    high, low = second
    rows = high.shape[0]
    a = mb(cat([high, low], axis=0), stack, NT)
    return a[:rows, :BS] + a[rows:, :BS] + a[:rows, BS:]


def second_term(stack, first):
    high, low = first
    rows = high.shape[0]
    left = cat([cat([high, high], axis=1), cat([low, jnp.zeros_like(low)], axis=1)], axis=0)
    b = mb(left, stack, NN)
    return b[:rows] + b[rows:]


def own_block(i, own_blocks):
    return lax.rem(i, own_blocks) if own_blocks & (own_blocks - 1) else i & (own_blocks - 1)


def start_kernel(wide, cap, own_blocks, pairs, points, q_in, unit_out, out, unit, raw, q, meta, sems, sem):
    vec_rows = q.shape[0]
    panels = raw.shape[1] // BS
    slot_rows = panels * BS + 2 * vec_rows
    size = raw.shape[0] // CHUNKS
    loads = [
        pltpu.make_async_copy(
            points.at[pl.ds(k * size, size), :], raw.at[pl.ds(k * size, size), :], sems.at[k]
        )
        for k in range(CHUNKS)
    ]
    loads.append(pltpu.make_async_copy(q_in, q, sems.at[CHUNKS]))
    for load in (loads[-1], *loads[:-1]):
        load.start()
    loads[-1].wait()
    high, low = split(q[...])
    for b in range(own_blocks):
        cols = slice(b * BS, (b + 1) * BS)
        unit[b, panels * BS :, :] = cat([high[:, cols], low[:, cols]], axis=0)
    half = own_blocks // 2
    for k in range(CHUNKS):
        loads[k].wait()
        for b in range(own_blocks // CHUNKS):
            x = raw[pl.ds(k * size + b * BS, BS), :].astype(F32)
            x = x * lax.rsqrt(jnp.sum(x * x, axis=-1, keepdims=True) + EPSILON)
            x = x.astype(BF)
            for h in range(panels):
                at = slice(h * BS, (h + 1) * BS)
                unit[k * (own_blocks // CHUNKS) + b, at, :] = x[:, at]
        if k % (CHUNKS // 2) != CHUNKS // 2 - 1:
            continue
        late = k == CHUNKS - 1

        def send(p, carry, late=late):
            for c in range(cap):
                i = own_block(pairs[0, p * cap + c], own_blocks)

                @pl.when((i >= half) == late)
                def _(i=i, c=c):
                    pltpu.make_async_copy(
                        unit.at[i], out.at[p, pl.ds(c * slot_rows, slot_rows), :], sem
                    ).start()

            return carry

        lax.fori_loop(0, wide, send, 0, unroll=8)
    keep = pltpu.make_async_copy(unit, unit_out, sems.at[CHUNKS + 1])
    keep.start()
    both = cat([high, low], axis=0)
    gram = mb(both, both, NT)
    gram = gram[:vec_rows, :vec_rows] + (gram[:vec_rows, vec_rows:] + gram[vec_rows:, :vec_rows])
    pieces = []
    for _ in range(3):
        pieces.append(gram.astype(BF).astype(F32))
        gram = gram - pieces[-1]
    sums = cat(pieces + [jnp.zeros((vec_rows, BS - 3 * vec_rows), F32)], axis=1)
    lanes = lax.broadcasted_iota(jnp.int32, sums.shape, 1)

    def label(p, carry):
        ids = [own_block(pairs[1, p * cap + c], own_blocks).astype(F32) for c in range(cap)]
        right = jnp.where(lanes < BS // 2 + BS // 4, ids[0], ids[1])
        meta[p] = jnp.where(lanes < BS // 2, sums, right).astype(BF)
        return carry

    lax.fori_loop(0, wide, label, 0, unroll=8)
    pltpu.make_async_copy(meta, out.at[:, pl.ds(cap * slot_rows, vec_rows), :], sem).start()
    pltpu.make_async_copy(out, out, sem).wait()
    keep.wait()


def put_terms(terms, ids, first_slot, cap, rows, back, total):
    for s, (to_first, to_second) in enumerate(terms):
        back[(first_slot + s) // cap, (s % cap) * rows : (s % cap + 1) * rows, :] = to_first
        total[:, block(ids[s])] += to_second


def tiles_kernel(peers, cap, sent, unit, q, tiles, back, total, gram, ids, got, labels, sems):
    wide = got.shape[0]
    vec_rows = q.shape[0]
    slot_rows = unit.shape[1]
    panels = (slot_rows - 2 * vec_rows) // BS
    slots = range(peers * cap)
    steps = wide // peers

    def load(k):
        part = pl.ds(k * peers, peers)
        here = pl.ds(0, cap * slot_rows)
        return pltpu.make_async_copy(sent.at[part, here], got.at[part], sems.at[k])

    first = pltpu.make_async_copy(
        sent.at[:, pl.ds(cap * slot_rows, vec_rows)], labels, sems.at[steps]
    )
    first.start()
    for k in range(steps):
        load(k).start()
    total[...] = jnp.zeros_like(total)
    first.wait()
    gram[...] = jnp.sum(labels[...].astype(F32), axis=0)
    for p in range(wide):
        label = labels[p].astype(F32)
        for c in range(cap):
            ids[p * cap + c] = label[0, BS // 2 + c * (BS // 4)].astype(jnp.int32)

    def chunk(k, carry):
        load(k).wait()
        peer = k * peers
        held = [ids[peer * cap + s] for s in slots]
        stacks = []
        for s in slots:
            at = (s % cap) * slot_rows
            here = [got[peer + s // cap, pl.ds(at + h * BS, BS), :] for h in range(panels)]
            own = [unit[held[s], h * BS : (h + 1) * BS, :] for h in range(panels)]
            inner = mb(cat(here, axis=1), cat(own, axis=1), NT)
            stacks.append(tile_stack(jnp.exp(KERNEL_FACTOR * (inner - 1.0))))
            tiles[peer * cap + s] = stacks[s]
        terms = []
        for s in slots:
            at = (s % cap) * slot_rows + panels * BS
            first = [got[peer + s // cap, pl.ds(at + h * vec_rows, vec_rows), :] for h in range(2)]
            second = split(q[:, block(held[s])])
            terms.append((first_term(stacks[s], second), second_term(stacks[s], first)))
        put_terms(terms, held, peer * cap, cap, vec_rows, back, total)
        return carry

    lax.fori_loop(0, steps, chunk, 0)


def gather_kernel(peers, cap, own_blocks, pairs, ids, got, tiles, top, low):
    half = top.shape[0]
    vec_rows = 2 * half
    slots = range(peers * cap)
    top[...] = jnp.zeros_like(top)
    low[...] = jnp.zeros_like(low)

    def put(at, term):
        top[:, at] += term[:half]
        low[:, at] += term[half:]

    def chunk(k, carry):
        peer = k * peers
        terms = []
        for s in slots:
            first = split(got[peer + s // cap, pl.ds((s % cap) * vec_rows, vec_rows), :])
            terms.append(second_term(tiles[peer * cap + s], first))
        for s in slots:
            put(block(ids[peer * cap + s]), terms[s])
            i = own_block(pairs[0, peer * cap + s], own_blocks)
            put(block(i), got[peer + s // cap, pl.ds((cap + s % cap) * vec_rows, vec_rows), :])
        return carry

    lax.fori_loop(0, got.shape[0] // peers, chunk, 0)


def sum_kernel(cap, own_blocks, pairs, got, total, top, low):
    vec_rows = total.shape[0]
    half = vec_rows // 2
    top[...] = total[:half]
    low[...] = total[half:]

    def add(p, carry):
        for c in range(cap):
            i = own_block(pairs[0, p * cap + c], own_blocks)
            top[:, block(i)] += got[p, c * vec_rows : c * vec_rows + half, :]
            low[:, block(i)] += got[p, c * vec_rows + half : (c + 1) * vec_rows, :]
        return carry

    lax.fori_loop(0, got.shape[0], add, 0, unroll=8)


def first_factor_kernel(points, gram, q_init, inverse, q):
    g = gram[...]
    n = q.shape[0]
    _, inv = factor_of((g[:, :n] + g[:, n : 2 * n] + g[:, 2 * n : 3 * n]) * (1.0 / points))
    inverse[...] = inv
    q[...] = apply_small(inv, q_init[...])


def factor_kernel(points, cap, got, w0, q, y, along, low_out, inverse, q_next, part, y_part):
    n = along.shape[0]
    a, low, inv, turned = step_matrices(got[:, 2 * cap * n :, :], points)
    along[...] = a
    low_out[...] = low
    inverse[...] = inv
    none = jnp.zeros_like(low)
    rows = lax.broadcasted_iota(jnp.int32, (n, n), 0)
    cols = lax.broadcasted_iota(jnp.int32, (n, n), 1)
    across = mm(-low, (rows == cols).astype(F32), TN)
    lines = [[inv, -turned, none], [none, none, -turned], [none, across, -turned]]
    matrix = cat([cat(line, axis=1) for line in lines], axis=0)
    new = apply_small(matrix, cat([w0[...], q[...], y[...]], axis=0))
    q_next[...] = new[:n]
    y_part[...] = new[n : 2 * n]
    part[...] = new[2 * n :]


def update_kernel(peers, cap, own_blocks, kept, pairs, ids, t0, t1, b0, b1, inverse, q, *refs):
    parts, rest = refs[:kept], refs[kept:]
    tiles, outs, out = (rest[0], rest[1:-1], rest[-1]) if cap else (None, rest[:-1], rest[-1])
    image = cat([t0[...] + t1[...], b0[...] + b1[...]], axis=0)
    n = image.shape[0]
    image = apply_small(inverse[...], image)
    w0 = outs[0]
    new = image + parts[0][...] if kept else image
    w0[...] = new
    if kept > 1:
        outs[1][...] = image + parts[1][...]
    tail = fold(q[...], new)
    if not cap:
        out[...] = jnp.broadcast_to(tail[None], out.shape)
        return

    def chunk(k, carry):
        peer = k * peers
        slots = range(peers * cap)
        terms = []
        for s in slots:
            second = split(w0[:, block(ids[peer * cap + s])])
            terms.append(first_term(tiles[peer * cap + s], second))
        for s in slots:
            p, c = peer + s // cap, s % cap
            i = own_block(pairs[0, peer * cap + s], own_blocks)
            out[p, c * n : (c + 1) * n, :] = w0[:, block(i)]
            out[p, (cap + c) * n : (cap + c + 1) * n, :] = terms[s]
        for p in range(peers):
            out[peer + p, 2 * cap * n :, :] = tail
        return carry

    lax.fori_loop(0, out.shape[0] // peers, chunk, 0)


def finish_kernel(points, got, w0, q, a0, l0, a1, l1, basis, coeffs):
    s, a, b = sums_of(got[...], points)
    n = a.shape[0]
    rows = lax.broadcasted_iota(jnp.int32, (n, n), 0)
    cols = lax.broadcasted_iota(jnp.int32, (n, n), 1)
    turned = mm(a, (rows == cols).astype(F32), TN)
    rest = w0[...] - apply_small(turned, q[...])
    low, inverse = factor_of(rest_gram(s, a, b))
    basis[...] = apply_small(inverse, rest)
    for k, m in enumerate((a0[...], l0[...], a1[...], l1[...], a, low)):
        coeffs[k // 2, k % 2] = m


def call(kernel, outs, n_ids=0, limit=VMEM_LIMIT, **more):
    params = pltpu.CompilerParams(vmem_limit_bytes=limit)
    shapes = tuple(jax.ShapeDtypeStruct(s, d) for s, d in outs)
    def run(*args):
        given = dict(more)
        vmem = pl.BlockSpec(memory_space=pltpu.VMEM)
        places = [pl.BlockSpec(memory_space=pltpu.SMEM)] * n_ids + [vmem] * (len(args) - n_ids)
        given.setdefault("in_specs", places)
        given.setdefault("out_specs", (vmem,) * len(outs))
        return pl.pallas_call(kernel, out_shape=shapes, compiler_params=params, **given)(*args)

    return run


def per_device(points, q_init, pairs):
    wide = lax.axis_size("wide")
    narrow = lax.axis_size("narrow")
    own_points, width = points.shape
    own_blocks = own_points // BS
    vec_rows = q_init.shape[0]
    pair_count = pairs.shape[1]
    cap = pair_count // wide
    total_points = own_points * wide
    slot_rows = width // BS * BS + 2 * vec_rows
    start_rows = cap * slot_rows + vec_rows
    peers = min(8, wide)
    vectors = ((vec_rows, own_points), F32)
    small = ((vec_rows, vec_rows), F32)
    payload = ((wide, 2 * cap * vec_rows + TAIL, BS), F32)
    reply = ((wide, cap * vec_rows, BS), F32)
    tail = ((wide, TAIL, BS), F32)

    def exchange(x):
        return lax.all_to_all(x, "wide", split_axis=0, concat_axis=0, tiled=True)

    anywhere = pl.BlockSpec(memory_space=pl.ANY)
    unit, sent = call(
        functools.partial(start_kernel, wide, cap, own_blocks),
        [((own_blocks, slot_rows, BS), BF), ((wide, start_rows, BS), BF)],
        1,
        VMEM_START,
        in_specs=[pl.BlockSpec(memory_space=pltpu.SMEM), anywhere, anywhere],
        out_specs=(anywhere, anywhere),
        scratch_shapes=[
            pltpu.VMEM((own_blocks, slot_rows, BS), BF),
            pltpu.VMEM((own_points, width), BF),
            pltpu.VMEM((vec_rows, own_points), F32),
            pltpu.VMEM((wide, vec_rows, BS), BF),
            pltpu.SemaphoreType.DMA((CHUNKS + 2,)),
            pltpu.SemaphoreType.DMA,
        ],
    )(pairs, points, q_init)
    vmem = pl.BlockSpec(memory_space=pltpu.VMEM)
    tiles, back, total, gram, ids = call(
        functools.partial(tiles_kernel, peers * 2, cap),
        [
            ((pair_count, 2 * BS, BS), BF),
            reply,
            vectors,
            ((vec_rows, BS), F32),
            ((pair_count,), jnp.int32),
        ],
        0,
        VMEM_TILES,
        in_specs=[anywhere, vmem, vmem],
        out_specs=(vmem, vmem, vmem, vmem, pl.BlockSpec(memory_space=pltpu.SMEM)),
        scratch_shapes=[
            pltpu.VMEM((wide, cap * slot_rows, BS), BF),
            pltpu.VMEM((wide, vec_rows, BS), BF),
            pltpu.SemaphoreType.DMA((wide // peers + 1,)),
        ],
    )(exchange(sent), unit, q_init)

    def swap(x, mask):
        return lax.ppermute(x, "narrow", [(i, i ^ mask) for i in range(narrow)])

    half = ((vec_rows // 2, own_points), F32)

    def narrow_sum(top, low):
        top_from, low_from = swap(top, 1), swap(low, 3)
        top, low = top + top_from, low + low_from
        return top, swap(top, 3), low, swap(low, 1)

    def update(kept, last, *args):
        count = max(kept, 1)
        return call(
            functools.partial(update_kernel, 4 * peers, 0 if last else cap, own_blocks, kept),
            [vectors] * count + [tail if last else payload],
            2,
        )(pairs, ids, *args, *([] if last else [tiles]))

    sums = narrow_sum(
        *call(functools.partial(sum_kernel, cap, own_blocks), [half, half], 1)(
            pairs, exchange(back), total
        )
    )
    inverse, q = call(
        functools.partial(first_factor_kernel, total_points), [small, vectors]
    )(gram, q_init)
    w0, out = update(0, False, *sums, inverse, q)
    y = w0
    records = []
    for step in range(1, STEPS):
        last = step == STEPS - 1
        got = exchange(out)
        sums = narrow_sum(
            *call(functools.partial(gather_kernel, 4 * peers, cap, own_blocks), [half, half], 2)(
                pairs, ids, got, tiles
            )
        )
        along, low, inverse, q, *parts = call(
            functools.partial(factor_kernel, total_points, cap),
            [small, small, small, vectors, vectors, vectors],
        )(got, w0, q, y)
        count = 1 if last else 2
        *new, out = update(count, last, *sums, inverse, q, *parts[:count])
        w0, y = new[0], new[-1]
        records += [along, low]
    return call(
        functools.partial(finish_kernel, total_points),
        [vectors, ((STEPS, 2, vec_rows, vec_rows), F32)],
    )(exchange(out), w0, q, *records)


def solution(mesh):
    placed = (P("wide", None), P(None, "wide"), P(None, ("wide", "narrow")))
    return jax.shard_map(
        per_device, mesh=mesh, in_specs=placed, out_specs=(P(None, "wide"), P()), check_vma=False
    )
```

```python
import functools

import jax
import jax.numpy as jnp
from jax import lax
from jax.experimental import pallas as pl
from jax.experimental.pallas import tpu as pltpu
from jax.sharding import PartitionSpec as P

BS = 128
STEPS = 3
KERNEL_FACTOR = 3.0
EPSILON = 1e-06
HIGH = lax.Precision.HIGHEST
VMEM_LIMIT = 16 * 2**20
VMEM_START = 60 * 2**20
VMEM_TILES = 30 * 2**20
TAIL = 8
CHUNKS = 4
BF = jnp.bfloat16
F32 = jnp.float32
NT = (((1,), (1,)), ((), ()))
TN = (((0,), (0,)), ((), ()))
NN = (((1,), (0,)), ((), ()))
cat = jnp.concatenate


def mm(a, b, dims):
    return lax.dot_general(a, b, dims, precision=HIGH, preferred_element_type=F32)


def mb(a, b, dims):
    return lax.dot_general(a, b, dims, preferred_element_type=F32)


def split(x):
    high = x.astype(BF)
    return high, (x - high.astype(F32)).astype(BF)


def block(i):
    return pl.ds(pl.multiple_of(i * BS, BS), BS)


def apply_small(m, x):
    rows = m.shape[0]
    m_high, m_low = split(m)
    left = cat([cat([m_high, m_high], axis=1), cat([m_low, jnp.zeros_like(m_low)], axis=1)], axis=0)
    out = mb(left, cat(split(x), axis=0), NN)
    return out[:rows] + out[rows:]


def factor_of(gram):
    n = gram.shape[0]
    rows = lax.broadcasted_iota(jnp.int32, (n, n), 0)
    cols = lax.broadcasted_iota(jnp.int32, (n, n), 1)
    same = (rows == cols).astype(F32)
    low, inverse, left = same, same, gram
    across, down = jnp.ones((1, n), F32), jnp.ones((n, 1), F32)
    for j in range(n):
        pivot = left[j : j + 1, j : j + 1]
        column = jnp.where(rows > j, left[:, j : j + 1] * (1.0 / pivot), 0.0)
        left = left - column * left[j : j + 1, :]
        inverse = inverse - column * inverse[j : j + 1, :]
        low = jnp.where(cols == j, low + column, low)
        across = jnp.where(cols[:1] == j, pivot, across)
        down = jnp.where(rows[:, :1] == j, pivot, down)
    return low * jnp.sqrt(across), inverse * (1.0 / jnp.sqrt(down))


def fold(q, w):
    n = q.shape[0]
    both = cat(split(cat([q, w], axis=0)), axis=0)
    g = mb(both, both, NT)
    g = g[: 2 * n, : 2 * n] + (g[: 2 * n, 2 * n :] + g[2 * n :, : 2 * n])
    parts = (g[:n, :n], g[:n, n:], g[n:, n:])
    pieces = [p[h : h + 8] for p in parts for h in (0, 8)]
    return cat(pieces + [jnp.zeros((8, BS - 6 * n), F32)], axis=1)


def sums_of(tails, points):
    t = jnp.sum(tails, axis=0) * (1.0 / points)
    return (cat([t[:, k : k + 16], t[:, k + 16 : k + 32]], axis=0) for k in (0, 32, 64))


def rest_gram(s, a, b):
    return b - mm(a, 2.0 * a - mm(s, a, NN), TN)


def step_matrices(tails, points):
    s, a, b = sums_of(tails, points)
    low, inverse = factor_of(rest_gram(s, a, b))
    return a, low, inverse, mm(inverse, a, NT)


def tile_stack(tile):
    return cat(split(tile), axis=0)


def first_term(stack, second):
    high, low = second
    rows = high.shape[0]
    a = mb(cat([high, low], axis=0), stack, NT)
    return a[:rows, :BS] + a[rows:, :BS] + a[:rows, BS:]


def second_term(stack, first):
    high, low = first
    rows = high.shape[0]
    left = cat([cat([high, high], axis=1), cat([low, jnp.zeros_like(low)], axis=1)], axis=0)
    b = mb(left, stack, NN)
    return b[:rows] + b[rows:]


def own_block(i, own_blocks):
    return lax.rem(i, own_blocks) if own_blocks & (own_blocks - 1) else i & (own_blocks - 1)


def start_kernel(wide, cap, own_blocks, pairs, points, q_in, unit_out, out, unit, raw, q, meta, sems, sem):
    vec_rows = q.shape[0]
    panels = raw.shape[1] // BS
    slot_rows = panels * BS + 2 * vec_rows
    size = raw.shape[0] // CHUNKS
    loads = [
        pltpu.make_async_copy(
            points.at[pl.ds(k * size, size), :], raw.at[pl.ds(k * size, size), :], sems.at[k]
        )
        for k in range(CHUNKS)
    ]
    loads.append(pltpu.make_async_copy(q_in, q, sems.at[CHUNKS]))
    for load in (loads[-1], *loads[:-1]):
        load.start()
    loads[-1].wait()
    high, low = split(q[...])
    for b in range(own_blocks):
        cols = slice(b * BS, (b + 1) * BS)
        unit[b, panels * BS :, :] = cat([high[:, cols], low[:, cols]], axis=0)
    half = own_blocks // 2
    for k in range(CHUNKS):
        loads[k].wait()
        for b in range(own_blocks // CHUNKS):
            x = raw[pl.ds(k * size + b * BS, BS), :].astype(F32)
            x = x * lax.rsqrt(jnp.sum(x * x, axis=-1, keepdims=True) + EPSILON)
            x = x.astype(BF)
            for h in range(panels):
                at = slice(h * BS, (h + 1) * BS)
                unit[k * (own_blocks // CHUNKS) + b, at, :] = x[:, at]
        if k % (CHUNKS // 2) != CHUNKS // 2 - 1:
            continue
        late = k == CHUNKS - 1

        def send(p, carry, late=late):
            for c in range(cap):
                i = own_block(pairs[0, p * cap + c], own_blocks)

                @pl.when((i >= half) == late)
                def _(i=i, c=c):
                    pltpu.make_async_copy(
                        unit.at[i], out.at[p, pl.ds(c * slot_rows, slot_rows), :], sem
                    ).start()

            return carry

        lax.fori_loop(0, wide, send, 0, unroll=8)
    keep = pltpu.make_async_copy(unit, unit_out, sems.at[CHUNKS + 1])
    keep.start()
    both = cat([high, low], axis=0)
    gram = mb(both, both, NT)
    gram = gram[:vec_rows, :vec_rows] + (gram[:vec_rows, vec_rows:] + gram[vec_rows:, :vec_rows])
    pieces = []
    for _ in range(3):
        pieces.append(gram.astype(BF).astype(F32))
        gram = gram - pieces[-1]
    sums = cat(pieces + [jnp.zeros((vec_rows, BS - 3 * vec_rows), F32)], axis=1)
    lanes = lax.broadcasted_iota(jnp.int32, sums.shape, 1)

    def label(p, carry):
        ids = [own_block(pairs[1, p * cap + c], own_blocks).astype(F32) for c in range(cap)]
        right = jnp.where(lanes < BS // 2 + BS // 4, ids[0], ids[1])
        meta[p] = jnp.where(lanes < BS // 2, sums, right).astype(BF)
        return carry

    lax.fori_loop(0, wide, label, 0, unroll=8)
    pltpu.make_async_copy(meta, out.at[:, pl.ds(cap * slot_rows, vec_rows), :], sem).start()
    pltpu.make_async_copy(out, out, sem).wait()
    keep.wait()


def put_terms(terms, ids, first_slot, cap, rows, back, total):
    for s, (to_first, to_second) in enumerate(terms):
        back[(first_slot + s) // cap, (s % cap) * rows : (s % cap + 1) * rows, :] = to_first
        total[:, block(ids[s])] += to_second


def tiles_kernel(peers, cap, got, unit, q, tiles, back, total, gram, ids):
    wide = got.shape[0]
    vec_rows = q.shape[0]
    slot_rows = unit.shape[1]
    panels = (slot_rows - 2 * vec_rows) // BS
    slots = range(peers * cap)
    steps = wide // peers

    total[...] = jnp.zeros_like(total)
    labels = got.at[:, pl.ds(cap * slot_rows, vec_rows), :]
    gram[...] = jnp.sum(labels[...].astype(F32), axis=0)
    for p in range(wide):
        label = labels[p].astype(F32)
        for c in range(cap):
            ids[p * cap + c] = label[0, BS // 2 + c * (BS // 4)].astype(jnp.int32)

    def chunk(k, carry):
        peer = k * peers
        held = [ids[peer * cap + s] for s in slots]
        stacks = []
        for s in slots:
            at = (s % cap) * slot_rows
            here = [got[peer + s // cap, pl.ds(at + h * BS, BS), :] for h in range(panels)]
            own = [unit[held[s], h * BS : (h + 1) * BS, :] for h in range(panels)]
            inner = mb(cat(here, axis=1), cat(own, axis=1), NT)
            stacks.append(tile_stack(jnp.exp(KERNEL_FACTOR * (inner - 1.0))))
            tiles[peer * cap + s] = stacks[s]
        terms = []
        for s in slots:
            at = (s % cap) * slot_rows + panels * BS
            first = [got[peer + s // cap, pl.ds(at + h * vec_rows, vec_rows), :] for h in range(2)]
            second = split(q[:, block(held[s])])
            terms.append((first_term(stacks[s], second), second_term(stacks[s], first)))
        put_terms(terms, held, peer * cap, cap, vec_rows, back, total)
        return carry

    lax.fori_loop(0, steps, chunk, 0)


def gather_kernel(peers, cap, own_blocks, pairs, ids, got, tiles, top, low):
    half = top.shape[0]
    vec_rows = 2 * half
    slots = range(peers * cap)
    top[...] = jnp.zeros_like(top)
    low[...] = jnp.zeros_like(low)

    def put(at, term):
        top[:, at] += term[:half]
        low[:, at] += term[half:]

    def chunk(k, carry):
        peer = k * peers
        terms = []
        for s in slots:
            first = split(got[peer + s // cap, pl.ds((s % cap) * vec_rows, vec_rows), :])
            terms.append(second_term(tiles[peer * cap + s], first))
        for s in slots:
            put(block(ids[peer * cap + s]), terms[s])
            i = own_block(pairs[0, peer * cap + s], own_blocks)
            put(block(i), got[peer + s // cap, pl.ds((cap + s % cap) * vec_rows, vec_rows), :])
        return carry

    lax.fori_loop(0, got.shape[0] // peers, chunk, 0)


def sum_kernel(cap, own_blocks, pairs, got, total, top, low):
    vec_rows = total.shape[0]
    half = vec_rows // 2
    top[...] = total[:half]
    low[...] = total[half:]

    def add(p, carry):
        for c in range(cap):
            i = own_block(pairs[0, p * cap + c], own_blocks)
            top[:, block(i)] += got[p, c * vec_rows : c * vec_rows + half, :]
            low[:, block(i)] += got[p, c * vec_rows + half : (c + 1) * vec_rows, :]
        return carry

    lax.fori_loop(0, got.shape[0], add, 0, unroll=8)


def first_factor_kernel(points, gram, q_init, inverse, q):
    g = gram[...]
    n = q.shape[0]
    _, inv = factor_of((g[:, :n] + g[:, n : 2 * n] + g[:, 2 * n : 3 * n]) * (1.0 / points))
    inverse[...] = inv
    q[...] = apply_small(inv, q_init[...])


def factor_kernel(points, cap, got, w0, q, y, along, low_out, inverse, q_next, part, y_part):
    n = along.shape[0]
    a, low, inv, turned = step_matrices(got[:, 2 * cap * n :, :], points)
    along[...] = a
    low_out[...] = low
    inverse[...] = inv
    none = jnp.zeros_like(low)
    rows = lax.broadcasted_iota(jnp.int32, (n, n), 0)
    cols = lax.broadcasted_iota(jnp.int32, (n, n), 1)
    across = mm(-low, (rows == cols).astype(F32), TN)
    lines = [[inv, -turned, none], [none, none, -turned], [none, across, -turned]]
    matrix = cat([cat(line, axis=1) for line in lines], axis=0)
    new = apply_small(matrix, cat([w0[...], q[...], y[...]], axis=0))
    q_next[...] = new[:n]
    y_part[...] = new[n : 2 * n]
    part[...] = new[2 * n :]


def update_kernel(peers, cap, own_blocks, kept, pairs, ids, t0, t1, b0, b1, inverse, q, *refs):
    parts, rest = refs[:kept], refs[kept:]
    tiles, outs, out = (rest[0], rest[1:-1], rest[-1]) if cap else (None, rest[:-1], rest[-1])
    image = cat([t0[...] + t1[...], b0[...] + b1[...]], axis=0)
    n = image.shape[0]
    image = apply_small(inverse[...], image)
    w0 = outs[0]
    new = image + parts[0][...] if kept else image
    w0[...] = new
    if kept > 1:
        outs[1][...] = image + parts[1][...]
    tail = fold(q[...], new)
    if not cap:
        out[...] = jnp.broadcast_to(tail[None], out.shape)
        return

    def chunk(k, carry):
        peer = k * peers
        slots = range(peers * cap)
        terms = []
        for s in slots:
            second = split(w0[:, block(ids[peer * cap + s])])
            terms.append(first_term(tiles[peer * cap + s], second))
        for s in slots:
            p, c = peer + s // cap, s % cap
            i = own_block(pairs[0, peer * cap + s], own_blocks)
            out[p, c * n : (c + 1) * n, :] = w0[:, block(i)]
            out[p, (cap + c) * n : (cap + c + 1) * n, :] = terms[s]
        for p in range(peers):
            out[peer + p, 2 * cap * n :, :] = tail
        return carry

    lax.fori_loop(0, out.shape[0] // peers, chunk, 0)


def finish_kernel(points, got, w0, q, a0, l0, a1, l1, basis, coeffs):
    s, a, b = sums_of(got[...], points)
    n = a.shape[0]
    rows = lax.broadcasted_iota(jnp.int32, (n, n), 0)
    cols = lax.broadcasted_iota(jnp.int32, (n, n), 1)
    turned = mm(a, (rows == cols).astype(F32), TN)
    rest = w0[...] - apply_small(turned, q[...])
    low, inverse = factor_of(rest_gram(s, a, b))
    basis[...] = apply_small(inverse, rest)
    for k, m in enumerate((a0[...], l0[...], a1[...], l1[...], a, low)):
        coeffs[k // 2, k % 2] = m


def call(kernel, outs, n_ids=0, limit=VMEM_LIMIT, **more):
    params = pltpu.CompilerParams(vmem_limit_bytes=limit)
    shapes = tuple(jax.ShapeDtypeStruct(s, d) for s, d in outs)
    def run(*args):
        given = dict(more)
        vmem = pl.BlockSpec(memory_space=pltpu.VMEM)
        places = [pl.BlockSpec(memory_space=pltpu.SMEM)] * n_ids + [vmem] * (len(args) - n_ids)
        given.setdefault("in_specs", places)
        given.setdefault("out_specs", (vmem,) * len(outs))
        return pl.pallas_call(kernel, out_shape=shapes, compiler_params=params, **given)(*args)

    return run


def per_device(points, q_init, pairs):
    wide = lax.axis_size("wide")
    narrow = lax.axis_size("narrow")
    own_points, width = points.shape
    own_blocks = own_points // BS
    vec_rows = q_init.shape[0]
    pair_count = pairs.shape[1]
    cap = pair_count // wide
    total_points = own_points * wide
    slot_rows = width // BS * BS + 2 * vec_rows
    start_rows = cap * slot_rows + vec_rows
    peers = min(8, wide)
    vectors = ((vec_rows, own_points), F32)
    small = ((vec_rows, vec_rows), F32)
    payload = ((wide, 2 * cap * vec_rows + TAIL, BS), F32)
    reply = ((wide, cap * vec_rows, BS), F32)
    tail = ((wide, TAIL, BS), F32)

    def exchange(x):
        return lax.all_to_all(x, "wide", split_axis=0, concat_axis=0, tiled=True)

    anywhere = pl.BlockSpec(memory_space=pl.ANY)
    unit, sent = call(
        functools.partial(start_kernel, wide, cap, own_blocks),
        [((own_blocks, slot_rows, BS), BF), ((wide, start_rows, BS), BF)],
        1,
        VMEM_START,
        in_specs=[pl.BlockSpec(memory_space=pltpu.SMEM), anywhere, anywhere],
        out_specs=(anywhere, anywhere),
        scratch_shapes=[
            pltpu.VMEM((own_blocks, slot_rows, BS), BF),
            pltpu.VMEM((own_points, width), BF),
            pltpu.VMEM((vec_rows, own_points), F32),
            pltpu.VMEM((wide, vec_rows, BS), BF),
            pltpu.SemaphoreType.DMA((CHUNKS + 2,)),
            pltpu.SemaphoreType.DMA,
        ],
    )(pairs, points, q_init)
    vmem = pl.BlockSpec(memory_space=pltpu.VMEM)
    tiles, back, total, gram, ids = call(
        functools.partial(tiles_kernel, peers * 4, cap),
        [
            ((pair_count, 2 * BS, BS), BF),
            reply,
            vectors,
            ((vec_rows, BS), F32),
            ((pair_count,), jnp.int32),
        ],
        0,
        VMEM_TILES,
        in_specs=[vmem, vmem, vmem],
        out_specs=(vmem, vmem, vmem, vmem, pl.BlockSpec(memory_space=pltpu.SMEM)),
    )(exchange(sent), unit, q_init)

    def swap(x, mask):
        return lax.ppermute(x, "narrow", [(i, i ^ mask) for i in range(narrow)])

    half = ((vec_rows // 2, own_points), F32)

    def narrow_sum(top, low):
        top_from, low_from = swap(top, 1), swap(low, 3)
        top, low = top + top_from, low + low_from
        return top, swap(top, 3), low, swap(low, 1)

    def update(kept, last, *args):
        count = max(kept, 1)
        return call(
            functools.partial(update_kernel, 4 * peers, 0 if last else cap, own_blocks, kept),
            [vectors] * count + [tail if last else payload],
            2,
        )(pairs, ids, *args, *([] if last else [tiles]))

    sums = narrow_sum(
        *call(functools.partial(sum_kernel, cap, own_blocks), [half, half], 1)(
            pairs, exchange(back), total
        )
    )
    inverse, q = call(
        functools.partial(first_factor_kernel, total_points), [small, vectors]
    )(gram, q_init)
    w0, out = update(0, False, *sums, inverse, q)
    y = w0
    records = []
    for step in range(1, STEPS):
        last = step == STEPS - 1
        got = exchange(out)
        sums = narrow_sum(
            *call(functools.partial(gather_kernel, 4 * peers, cap, own_blocks), [half, half], 2)(
                pairs, ids, got, tiles
            )
        )
        along, low, inverse, q, *parts = call(
            functools.partial(factor_kernel, total_points, cap),
            [small, small, small, vectors, vectors, vectors],
        )(got, w0, q, y)
        count = 1 if last else 2
        *new, out = update(count, last, *sums, inverse, q, *parts[:count])
        w0, y = new[0], new[-1]
        records += [along, low]
    return call(
        functools.partial(finish_kernel, total_points),
        [vectors, ((STEPS, 2, vec_rows, vec_rows), F32)],
    )(exchange(out), w0, q, *records)


def solution(mesh):
    placed = (P("wide", None), P(None, "wide"), P(None, ("wide", "narrow")))
    return jax.shard_map(
        per_device, mesh=mesh, in_specs=placed, out_specs=(P(None, "wide"), P()), check_vma=False
    )
```

```python
import functools

import jax
import jax.numpy as jnp
from jax import lax
from jax.experimental import pallas as pl
from jax.experimental.pallas import tpu as pltpu
from jax.sharding import PartitionSpec as P

BS = 128
STEPS = 3
KERNEL_FACTOR = 3.0
EPSILON = 1e-06
HIGH = lax.Precision.HIGHEST
VMEM_LIMIT = 16 * 2**20
VMEM_START = 60 * 2**20
VMEM_TILES = 30 * 2**20
TAIL = 8
CHUNKS = 4
BF = jnp.bfloat16
F32 = jnp.float32
NT = (((1,), (1,)), ((), ()))
TN = (((0,), (0,)), ((), ()))
NN = (((1,), (0,)), ((), ()))
cat = jnp.concatenate


def mm(a, b, dims):
    return lax.dot_general(a, b, dims, precision=HIGH, preferred_element_type=F32)


def mb(a, b, dims):
    return lax.dot_general(a, b, dims, preferred_element_type=F32)


def split(x):
    high = x.astype(BF)
    return high, (x - high.astype(F32)).astype(BF)


def block(i):
    return pl.ds(pl.multiple_of(i * BS, BS), BS)


def apply_small(m, x):
    rows = m.shape[0]
    m_high, m_low = split(m)
    left = cat([cat([m_high, m_high], axis=1), cat([m_low, m_low], axis=1)], axis=0)
    out = mb(left, cat(split(x), axis=0), NN)
    return out[:rows] + out[rows:]


def factor_of(gram):
    n = gram.shape[0]
    rows = lax.broadcasted_iota(jnp.int32, (n, n), 0)
    cols = lax.broadcasted_iota(jnp.int32, (n, n), 1)
    same = (rows == cols).astype(F32)
    low, inverse, left = same, same, gram
    across, down = jnp.ones((1, n), F32), jnp.ones((n, 1), F32)
    for j in range(n):
        pivot = left[j : j + 1, j : j + 1]
        column = jnp.where(rows > j, left[:, j : j + 1] * (1.0 / pivot), 0.0)
        left = left - column * left[j : j + 1, :]
        inverse = inverse - column * inverse[j : j + 1, :]
        low = jnp.where(cols == j, low + column, low)
        across = jnp.where(cols[:1] == j, pivot, across)
        down = jnp.where(rows[:, :1] == j, pivot, down)
    return low * jnp.sqrt(across), inverse * (1.0 / jnp.sqrt(down))


def fold(q, w):
    n = q.shape[0]
    both = cat(split(cat([q, w], axis=0)), axis=0)
    g = mb(both, both, NT)
    m = 2 * n
    g = g[:m, :m] + (g[:m, m:] + g[m:, :m] + g[m:, m:])
    parts = (g[:n, :n], g[:n, n:], g[n:, n:])
    pieces = [p[h : h + 8] for p in parts for h in (0, 8)]
    return cat(pieces + [jnp.zeros((8, BS - 6 * n), F32)], axis=1)


def sums_of(tails, points):
    t = jnp.sum(tails, axis=0) * (1.0 / points)
    return (cat([t[:, k : k + 16], t[:, k + 16 : k + 32]], axis=0) for k in (0, 32, 64))


def rest_gram(s, a, b):
    return b - mm(a, 2.0 * a - mm(s, a, NN), TN)


def step_matrices(tails, points):
    s, a, b = sums_of(tails, points)
    low, inverse = factor_of(rest_gram(s, a, b))
    return a, low, inverse, mm(inverse, a, NT)


def tile_stack(tile):
    return cat(split(tile), axis=0)


def first_term(stack, second):
    high, low = second
    rows = high.shape[0]
    a = mb(cat([high, low], axis=0), stack, NT)
    return a[:rows, :BS] + (a[rows:, :BS] + a[:rows, BS:] + a[rows:, BS:])


def second_term(stack, first):
    high, low = first
    rows = high.shape[0]
    left = cat([cat([high, high], axis=1), cat([low, low], axis=1)], axis=0)
    b = mb(left, stack, NN)
    return b[:rows] + b[rows:]


def own_block(i, own_blocks):
    return lax.rem(i, own_blocks) if own_blocks & (own_blocks - 1) else i & (own_blocks - 1)


def start_kernel(wide, cap, own_blocks, pairs, points, q_in, unit_out, out, unit, raw, q, meta, sems, sem):
    vec_rows = q.shape[0]
    panels = raw.shape[1] // BS
    slot_rows = panels * BS + 2 * vec_rows
    size = raw.shape[0] // CHUNKS
    loads = [
        pltpu.make_async_copy(
            points.at[pl.ds(k * size, size), :], raw.at[pl.ds(k * size, size), :], sems.at[k]
        )
        for k in range(CHUNKS)
    ]
    loads.append(pltpu.make_async_copy(q_in, q, sems.at[CHUNKS]))
    for load in (loads[-1], *loads[:-1]):
        load.start()
    loads[-1].wait()
    high, low = split(q[...])
    for b in range(own_blocks):
        cols = slice(b * BS, (b + 1) * BS)
        unit[b, panels * BS :, :] = cat([high[:, cols], low[:, cols]], axis=0)
    half = own_blocks // 2
    for k in range(CHUNKS):
        loads[k].wait()
        for b in range(own_blocks // CHUNKS):
            x = raw[pl.ds(k * size + b * BS, BS), :].astype(F32)
            x = x * lax.rsqrt(jnp.sum(x * x, axis=-1, keepdims=True) + EPSILON)
            x = x.astype(BF)
            for h in range(panels):
                at = slice(h * BS, (h + 1) * BS)
                unit[k * (own_blocks // CHUNKS) + b, at, :] = x[:, at]
        if k % (CHUNKS // 2) != CHUNKS // 2 - 1:
            continue
        late = k == CHUNKS - 1

        def send(p, carry, late=late):
            for c in range(cap):
                i = own_block(pairs[0, p * cap + c], own_blocks)

                @pl.when((i >= half) == late)
                def _(i=i, c=c):
                    pltpu.make_async_copy(
                        unit.at[i], out.at[p, pl.ds(c * slot_rows, slot_rows), :], sem
                    ).start()

            return carry

        lax.fori_loop(0, wide, send, 0, unroll=8)
    keep = pltpu.make_async_copy(unit, unit_out, sems.at[CHUNKS + 1])
    keep.start()
    both = cat([high, low], axis=0)
    gram = mb(both, both, NT)
    n = vec_rows
    gram = gram[:n, :n] + (gram[:n, n:] + gram[n:, :n] + gram[n:, n:])
    pieces = []
    for _ in range(3):
        pieces.append(gram.astype(BF).astype(F32))
        gram = gram - pieces[-1]
    sums = cat(pieces + [jnp.zeros((vec_rows, BS - 3 * vec_rows), F32)], axis=1)
    lanes = lax.broadcasted_iota(jnp.int32, sums.shape, 1)

    def label(p, carry):
        ids = [own_block(pairs[1, p * cap + c], own_blocks).astype(F32) for c in range(cap)]
        right = jnp.where(lanes < BS // 2 + BS // 4, ids[0], ids[1])
        meta[p] = jnp.where(lanes < BS // 2, sums, right).astype(BF)
        return carry

    lax.fori_loop(0, wide, label, 0, unroll=8)
    pltpu.make_async_copy(meta, out.at[:, pl.ds(cap * slot_rows, vec_rows), :], sem).start()
    pltpu.make_async_copy(out, out, sem).wait()
    keep.wait()


def put_terms(terms, ids, first_slot, cap, rows, back, total):
    for s, (to_first, to_second) in enumerate(terms):
        back[(first_slot + s) // cap, (s % cap) * rows : (s % cap + 1) * rows, :] = to_first
        total[:, block(ids[s])] += to_second


def tiles_kernel(peers, cap, got, unit, q, tiles, back, total, gram, ids):
    wide = got.shape[0]
    vec_rows = q.shape[0]
    slot_rows = unit.shape[1]
    panels = (slot_rows - 2 * vec_rows) // BS
    slots = range(peers * cap)
    steps = wide // peers

    total[...] = jnp.zeros_like(total)
    labels = got.at[:, pl.ds(cap * slot_rows, vec_rows), :]
    gram[...] = jnp.sum(labels[...].astype(F32), axis=0)
    for p in range(wide):
        label = labels[p].astype(F32)
        for c in range(cap):
            ids[p * cap + c] = label[0, BS // 2 + c * (BS // 4)].astype(jnp.int32)

    def chunk(k, carry):
        peer = k * peers
        held = [ids[peer * cap + s] for s in slots]
        stacks = []
        for s in slots:
            at = (s % cap) * slot_rows
            here = [got[peer + s // cap, pl.ds(at + h * BS, BS), :] for h in range(panels)]
            own = [unit[held[s], h * BS : (h + 1) * BS, :] for h in range(panels)]
            inner = mb(cat(here, axis=1), cat(own, axis=1), NT)
            stacks.append(tile_stack(jnp.exp(KERNEL_FACTOR * (inner - 1.0))))
            tiles[peer * cap + s] = stacks[s]
        terms = []
        for s in slots:
            at = (s % cap) * slot_rows + panels * BS
            first = [got[peer + s // cap, pl.ds(at + h * vec_rows, vec_rows), :] for h in range(2)]
            second = split(q[:, block(held[s])])
            terms.append((first_term(stacks[s], second), second_term(stacks[s], first)))
        put_terms(terms, held, peer * cap, cap, vec_rows, back, total)
        return carry

    lax.fori_loop(0, steps, chunk, 0)


def gather_kernel(peers, cap, own_blocks, pairs, ids, got, tiles, top, low):
    half = top.shape[0]
    vec_rows = 2 * half
    slots = range(peers * cap)
    top[...] = jnp.zeros_like(top)
    low[...] = jnp.zeros_like(low)

    def put(at, term):
        top[:, at] += term[:half]
        low[:, at] += term[half:]

    def chunk(k, carry):
        peer = k * peers
        terms = []
        for s in slots:
            first = split(got[peer + s // cap, pl.ds((s % cap) * vec_rows, vec_rows), :])
            terms.append(second_term(tiles[peer * cap + s], first))
        for s in slots:
            put(block(ids[peer * cap + s]), terms[s])
            i = own_block(pairs[0, peer * cap + s], own_blocks)
            put(block(i), got[peer + s // cap, pl.ds((cap + s % cap) * vec_rows, vec_rows), :])
        return carry

    lax.fori_loop(0, got.shape[0] // peers, chunk, 0)


def sum_kernel(cap, own_blocks, pairs, got, total, top, low):
    vec_rows = total.shape[0]
    half = vec_rows // 2
    top[...] = total[:half]
    low[...] = total[half:]

    def add(p, carry):
        for c in range(cap):
            i = own_block(pairs[0, p * cap + c], own_blocks)
            top[:, block(i)] += got[p, c * vec_rows : c * vec_rows + half, :]
            low[:, block(i)] += got[p, c * vec_rows + half : (c + 1) * vec_rows, :]
        return carry

    lax.fori_loop(0, got.shape[0], add, 0, unroll=8)


def first_factor_kernel(points, gram, q_init, inverse, q):
    g = gram[...]
    n = q.shape[0]
    _, inv = factor_of((g[:, :n] + g[:, n : 2 * n] + g[:, 2 * n : 3 * n]) * (1.0 / points))
    inverse[...] = inv
    q[...] = apply_small(inv, q_init[...])


def factor_kernel(points, cap, got, w0, q, y, along, low_out, inverse, q_next, part, y_part):
    n = along.shape[0]
    a, low, inv, turned = step_matrices(got[:, 2 * cap * n :, :], points)
    along[...] = a
    low_out[...] = low
    inverse[...] = inv
    none = jnp.zeros_like(low)
    rows = lax.broadcasted_iota(jnp.int32, (n, n), 0)
    cols = lax.broadcasted_iota(jnp.int32, (n, n), 1)
    across = mm(-low, (rows == cols).astype(F32), TN)
    lines = [[inv, -turned, none], [none, none, -turned], [none, across, -turned]]
    matrix = cat([cat(line, axis=1) for line in lines], axis=0)
    new = apply_small(matrix, cat([w0[...], q[...], y[...]], axis=0))
    q_next[...] = new[:n]
    y_part[...] = new[n : 2 * n]
    part[...] = new[2 * n :]


def update_kernel(peers, cap, own_blocks, kept, pairs, ids, t0, t1, b0, b1, inverse, q, *refs):
    parts, rest = refs[:kept], refs[kept:]
    tiles, outs, out = (rest[0], rest[1:-1], rest[-1]) if cap else (None, rest[:-1], rest[-1])
    image = cat([t0[...] + t1[...], b0[...] + b1[...]], axis=0)
    n = image.shape[0]
    image = apply_small(inverse[...], image)
    w0 = outs[0]
    new = image + parts[0][...] if kept else image
    w0[...] = new
    if kept > 1:
        outs[1][...] = image + parts[1][...]
    tail = fold(q[...], new)
    if not cap:
        out[...] = jnp.broadcast_to(tail[None], out.shape)
        return

    def chunk(k, carry):
        peer = k * peers
        slots = range(peers * cap)
        terms = []
        for s in slots:
            second = split(w0[:, block(ids[peer * cap + s])])
            terms.append(first_term(tiles[peer * cap + s], second))
        for s in slots:
            p, c = peer + s // cap, s % cap
            i = own_block(pairs[0, peer * cap + s], own_blocks)
            out[p, c * n : (c + 1) * n, :] = w0[:, block(i)]
            out[p, (cap + c) * n : (cap + c + 1) * n, :] = terms[s]
        for p in range(peers):
            out[peer + p, 2 * cap * n :, :] = tail
        return carry

    lax.fori_loop(0, out.shape[0] // peers, chunk, 0)


def finish_kernel(points, got, w0, q, a0, l0, a1, l1, basis, coeffs):
    s, a, b = sums_of(got[...], points)
    n = a.shape[0]
    rows = lax.broadcasted_iota(jnp.int32, (n, n), 0)
    cols = lax.broadcasted_iota(jnp.int32, (n, n), 1)
    turned = mm(a, (rows == cols).astype(F32), TN)
    rest = w0[...] - apply_small(turned, q[...])
    low, inverse = factor_of(rest_gram(s, a, b))
    basis[...] = apply_small(inverse, rest)
    for k, m in enumerate((a0[...], l0[...], a1[...], l1[...], a, low)):
        coeffs[k // 2, k % 2] = m


def call(kernel, outs, n_ids=0, limit=VMEM_LIMIT, **more):
    params = pltpu.CompilerParams(vmem_limit_bytes=limit)
    shapes = tuple(jax.ShapeDtypeStruct(s, d) for s, d in outs)
    def run(*args):
        given = dict(more)
        vmem = pl.BlockSpec(memory_space=pltpu.VMEM)
        places = [pl.BlockSpec(memory_space=pltpu.SMEM)] * n_ids + [vmem] * (len(args) - n_ids)
        given.setdefault("in_specs", places)
        given.setdefault("out_specs", (vmem,) * len(outs))
        return pl.pallas_call(kernel, out_shape=shapes, compiler_params=params, **given)(*args)

    return run


def per_device(points, q_init, pairs):
    wide = lax.axis_size("wide")
    narrow = lax.axis_size("narrow")
    own_points, width = points.shape
    own_blocks = own_points // BS
    vec_rows = q_init.shape[0]
    pair_count = pairs.shape[1]
    cap = pair_count // wide
    total_points = own_points * wide
    slot_rows = width // BS * BS + 2 * vec_rows
    start_rows = cap * slot_rows + vec_rows
    peers = min(8, wide)
    vectors = ((vec_rows, own_points), F32)
    small = ((vec_rows, vec_rows), F32)
    payload = ((wide, 2 * cap * vec_rows + TAIL, BS), F32)
    reply = ((wide, cap * vec_rows, BS), F32)
    tail = ((wide, TAIL, BS), F32)

    def exchange(x):
        return lax.all_to_all(x, "wide", split_axis=0, concat_axis=0, tiled=True)

    anywhere = pl.BlockSpec(memory_space=pl.ANY)
    unit, sent = call(
        functools.partial(start_kernel, wide, cap, own_blocks),
        [((own_blocks, slot_rows, BS), BF), ((wide, start_rows, BS), BF)],
        1,
        VMEM_START,
        in_specs=[pl.BlockSpec(memory_space=pltpu.SMEM), anywhere, anywhere],
        out_specs=(anywhere, anywhere),
        scratch_shapes=[
            pltpu.VMEM((own_blocks, slot_rows, BS), BF),
            pltpu.VMEM((own_points, width), BF),
            pltpu.VMEM((vec_rows, own_points), F32),
            pltpu.VMEM((wide, vec_rows, BS), BF),
            pltpu.SemaphoreType.DMA((CHUNKS + 2,)),
            pltpu.SemaphoreType.DMA,
        ],
    )(pairs, points, q_init)
    vmem = pl.BlockSpec(memory_space=pltpu.VMEM)
    tiles, back, total, gram, ids = call(
        functools.partial(tiles_kernel, peers * 4, cap),
        [
            ((pair_count, 2 * BS, BS), BF),
            reply,
            vectors,
            ((vec_rows, BS), F32),
            ((pair_count,), jnp.int32),
        ],
        0,
        VMEM_TILES,
        in_specs=[vmem, vmem, vmem],
        out_specs=(vmem, vmem, vmem, vmem, pl.BlockSpec(memory_space=pltpu.SMEM)),
    )(exchange(sent), unit, q_init)

    def swap(x, mask):
        return lax.ppermute(x, "narrow", [(i, i ^ mask) for i in range(narrow)])

    half = ((vec_rows // 2, own_points), F32)

    def narrow_sum(top, low):
        top_from, low_from = swap(top, 1), swap(low, 3)
        top, low = top + top_from, low + low_from
        return top, swap(top, 3), low, swap(low, 1)

    def update(kept, last, *args):
        count = max(kept, 1)
        return call(
            functools.partial(update_kernel, 4 * peers, 0 if last else cap, own_blocks, kept),
            [vectors] * count + [tail if last else payload],
            2,
        )(pairs, ids, *args, *([] if last else [tiles]))

    sums = narrow_sum(
        *call(functools.partial(sum_kernel, cap, own_blocks), [half, half], 1)(
            pairs, exchange(back), total
        )
    )
    inverse, q = call(
        functools.partial(first_factor_kernel, total_points), [small, vectors]
    )(gram, q_init)
    w0, out = update(0, False, *sums, inverse, q)
    y = w0
    records = []
    for step in range(1, STEPS):
        last = step == STEPS - 1
        got = exchange(out)
        sums = narrow_sum(
            *call(functools.partial(gather_kernel, 4 * peers, cap, own_blocks), [half, half], 2)(
                pairs, ids, got, tiles
            )
        )
        along, low, inverse, q, *parts = call(
            functools.partial(factor_kernel, total_points, cap),
            [small, small, small, vectors, vectors, vectors],
        )(got, w0, q, y)
        count = 1 if last else 2
        *new, out = update(count, last, *sums, inverse, q, *parts[:count])
        w0, y = new[0], new[-1]
        records += [along, low]
    return call(
        functools.partial(finish_kernel, total_points),
        [vectors, ((STEPS, 2, vec_rows, vec_rows), F32)],
    )(exchange(out), w0, q, *records)


def solution(mesh):
    placed = (P("wide", None), P(None, "wide"), P(None, ("wide", "narrow")))
    return jax.shard_map(
        per_device, mesh=mesh, in_specs=placed, out_specs=(P(None, "wide"), P()), check_vma=False
    )
```
